128 devices in a mesh: row: 8 (over x, y_lo), col: 16 (over y_hi, z, core).
Axes of the slice: x: 4, y: 4 (y_hi: 2, y_lo: 2; y = y_hi * 2 + y_lo), z: 4, core: 2. Of those that a mesh axis runs over, the one named last changes fastest.
Arguments:
- features: bfloat16 [128, 2048, 128], P('row', 'col'), may hold values from -6 to 6
- cotangent: bfloat16 [128, 2048, 128], P('row', 'col'), may hold values from -6 to 6
- w_in: bfloat16 [128, 256], replicated, may hold values from -0.5 to 0.5
- grid_in: bfloat16 [128, 256], replicated, may hold values from -0.5 to 0.5
- grid_mix: bfloat16 [256, 256], replicated, may hold values from -0.375 to 0.375
- grid_out: bfloat16 [128, 128], replicated, may hold values from -0.5 to 0.5
- block_in: bfloat16 [128, 256], replicated, may hold values from -0.5 to 0.5
- block_mix: bfloat16 [256, 256], replicated, may hold values from -0.375 to 0.375
- block_out: bfloat16 [128, 128], replicated, may hold values from -0.5 to 0.5
- w_out: bfloat16 [256, 128], replicated, may hold values from -0.375 to 0.375
Outputs:
- result: bfloat16 [128, 2048, 128], P('row', 'col')
- feature_grad: bfloat16 [128, 2048, 128], P('row', 'col')
- grad_w_in: float32 [128, 256], replicated
- grad_grid_in: float32 [128, 256], replicated
- grad_grid_mix: float32 [256, 256], replicated
- grad_grid_out: float32 [128, 128], replicated
- grad_block_in: float32 [128, 256], replicated
- grad_block_mix: float32 [256, 256], replicated
- grad_block_out: float32 [128, 128], replicated
- grad_w_out: float32 [256, 128], replicated
The draws below stay inside these ranges and needn't reach their ends.
All inputs are finite; a program needn't handle non-finite values.
Results may differ from the reference program's by a relative error of at most 0.012.
Values may be sent and summed in bfloat16 or wider, within the bound.
A program may use at most 128 MiB of HBM per device.

```python
import math
import jax
import jax.numpy as jnp
from jax import lax

CH = 128
GRID = 16
BLK = 16
H = 128
W = 2048


def block_levels(rng, shape, split, least, largest):
    def one(axis_at, parts):
        heights = jax.random.uniform(jax.random.fold_in(jax.random.fold_in(rng, 6), axis_at), (parts,), jnp.float32, least / len(split), largest / len(split))
        return jnp.repeat(jnp.exp(heights), shape[axis_at] // parts).reshape((-1,) + (1,) * (len(shape) - axis_at - 1))

    factor_of = one(*split[0])
    for cut in split[1:]:
        factor_of = factor_of * one(*cut)
    return factor_of


def gaussian(own_key, dims, width, limit, pieces=(), kind=jnp.bfloat16):
    drawn = width * jax.random.normal(own_key, dims, jnp.float32)
    if pieces:
        drawn = drawn * block_levels(own_key, dims, pieces, -0.22, 0.18)
    return jnp.clip(drawn, -limit, limit).astype(kind)


def setup_inputs(seed: int = 0) -> dict:
    streams_of = jax.random.split(jax.random.key(seed), 11)
    features = gaussian(streams_of[0], (H, W, CH), 1.0, 6.0, ((0, 8), (1, 16)))
    cotangent = gaussian(streams_of[1], (H, W, CH), 1.0, 6.0, ((0, 8), (1, 16)))
    w_in = gaussian(streams_of[2], (CH, 2 * CH), CH ** -0.5, 0.5)
    grid_in = gaussian(streams_of[3], (CH, 2 * CH), CH ** -0.5, 0.5)
    grid_mix = gaussian(streams_of[4], (GRID * GRID, GRID * GRID), (GRID * GRID) ** -0.5, 0.375)
    grid_out = gaussian(streams_of[5], (CH, CH), CH ** -0.5, 0.5)
    block_in = gaussian(streams_of[6], (CH, 2 * CH), CH ** -0.5, 0.5)
    block_mix = gaussian(streams_of[7], (BLK * BLK, BLK * BLK), (BLK * BLK) ** -0.5, 0.375)
    block_out = gaussian(streams_of[8], (CH, CH), CH ** -0.5, 0.5)
    w_out = gaussian(streams_of[9], (2 * CH, CH), (2 * CH) ** -0.5, 0.375)
    return dict(features=features, cotangent=cotangent, w_in=w_in, grid_in=grid_in, grid_mix=grid_mix, grid_out=grid_out, block_in=block_in, block_mix=block_mix, block_out=block_out, w_out=w_out)


epsilon = 1e-06
tanh_scale = 0.7978845608028654
cubic = 0.044715

def gelu_value(hidden):
    inner = jnp.tanh(tanh_scale * (hidden + cubic * hidden * hidden * hidden))
    return 0.5 * hidden * (1.0 + inner)

def gelu_slope(hidden):
    inner = jnp.tanh(tanh_scale * (hidden + cubic * hidden * hidden * hidden))
    return 0.5 * (1.0 + inner) + 0.5 * hidden * (1.0 - inner * inner) * tanh_scale * (1.0 + 3.0 * cubic * hidden * hidden)

def normalize(values):
    center = values - lax.optimization_barrier(jnp.mean(values, axis=-1, keepdims=True))
    spread = lax.rsqrt(lax.optimization_barrier(jnp.mean(center * center, axis=-1, keepdims=True)) + epsilon)
    return (center * spread, spread)

def normalize_back(upstream, unit, spread):
    return spread * (upstream - lax.optimization_barrier(jnp.mean(upstream, axis=-1, keepdims=True)) - unit * lax.optimization_barrier(jnp.mean(upstream * unit, axis=-1, keepdims=True)))

def matmul(left, right):
    return jnp.dot(left, right, preferred_element_type=jnp.float32)

def gram_sum(left, right):
    return lax.dot_general(left, right, (((0,), (0,)), ((), ())), preferred_element_type=jnp.float32)

def grid_apply(values, weight, transposed):
    blocks = values.astype(jnp.float32).reshape(GRID, H // GRID, GRID, W // GRID, CH)
    table = weight.astype(jnp.float32).reshape(GRID, GRID, GRID, GRID)
    form = 'xyab,xiyjc->aibjc' if transposed else 'abxy,xiyjc->aibjc'
    return jnp.einsum(form, table, blocks).reshape(H * W, CH)

def grid_grad(upstream, values):
    first = upstream.astype(jnp.float32).reshape(GRID, H // GRID, GRID, W // GRID, CH)
    second = values.astype(jnp.float32).reshape(GRID, H // GRID, GRID, W // GRID, CH)
    return jnp.einsum('aibjc,xiyjc->abxy', first, second).reshape(GRID * GRID, GRID * GRID)

def block_apply(values, weight, transposed):
    blocks = values.astype(jnp.float32).reshape(H // BLK, BLK, W // BLK, BLK, CH)
    table = weight.astype(jnp.float32).reshape(BLK, BLK, BLK, BLK)
    form = 'klij,akblc->aibjc' if transposed else 'ijkl,akblc->aibjc'
    return jnp.einsum(form, table, blocks).reshape(H * W, CH)

def block_grad(upstream, values):
    first = upstream.astype(jnp.float32).reshape(H // BLK, BLK, W // BLK, BLK, CH)
    second = values.astype(jnp.float32).reshape(H // BLK, BLK, W // BLK, BLK, CH)
    return jnp.einsum('aibjc,akblc->ijkl', first, second).reshape(BLK * BLK, BLK * BLK)

def branch_forward(inputs, in_weight, mix_weight, out_weight, applier):
    unit, spread = normalize(inputs.astype(jnp.float32))
    normed = unit.astype(jnp.bfloat16)
    hidden = matmul(normed, in_weight)
    activated = gelu_value(hidden)
    gate_part = activated[:, :CH]
    mix_unit, mix_spread = normalize(activated[:, CH:])
    mix_input = mix_unit.astype(jnp.bfloat16)
    mixed = applier(mix_input, mix_weight, False).astype(jnp.bfloat16)
    gated = (gate_part * (mixed.astype(jnp.float32) + 1.0)).astype(jnp.bfloat16)
    outcome = (inputs.astype(jnp.float32) + matmul(gated, out_weight)).astype(jnp.bfloat16)
    return (outcome, (unit, spread, normed, hidden, mix_unit, mix_spread, mix_input, mixed, gated))

def branch_backward(upstream, in_weight, mix_weight, out_weight, saved, applier, grader, factor):
    unit, spread, normed, hidden, mix_unit, mix_spread, mix_input, mixed, gated = saved
    grad_out = gram_sum(gated, upstream) * factor
    d_gated = matmul(upstream, out_weight.T)
    gate_part = gelu_value(hidden[:, :CH])
    d_gate = d_gated * (mixed.astype(jnp.float32) + 1.0)
    d_mixed = (d_gated * gate_part).astype(jnp.bfloat16)
    d_mix_input = applier(d_mixed, mix_weight, True).astype(jnp.bfloat16)
    grad_mix = grader(d_mixed, mix_input) * factor
    d_branch = normalize_back(d_mix_input.astype(jnp.float32), mix_unit, mix_spread)
    d_hidden = (jnp.concatenate([d_gate, d_branch], axis=-1) * gelu_slope(hidden)).astype(jnp.bfloat16)
    grad_in = gram_sum(normed, d_hidden) * factor
    d_inputs = upstream.astype(jnp.float32) + normalize_back(matmul(d_hidden, in_weight.T), unit, spread)
    return (d_inputs, grad_in, grad_mix, grad_out)

def reference(features, cotangent, w_in, grid_in, grid_mix, grid_out, block_in, block_mix, block_out, w_out):
    factor = 1.0 / math.sqrt(H * W)
    flat_in = features.reshape(H * W, CH)
    first_unit, first_spread = normalize(flat_in.astype(jnp.float32))
    first_normed = first_unit.astype(jnp.bfloat16)
    first_hidden = matmul(first_normed, w_in)
    first_active = gelu_value(first_hidden).astype(jnp.bfloat16)
    grid_result, grid_saved = branch_forward(first_active[:, :CH], grid_in, grid_mix, grid_out, grid_apply)
    block_result, block_saved = branch_forward(first_active[:, CH:], block_in, block_mix, block_out, block_apply)
    joined = jnp.concatenate([grid_result, block_result], axis=-1)
    result = (flat_in.astype(jnp.float32) + matmul(joined, w_out)).astype(jnp.bfloat16)
    flat_cot = cotangent.reshape(H * W, CH)
    grad_w_out = gram_sum(joined, flat_cot) * factor
    upstream = matmul(flat_cot, w_out.T).astype(jnp.bfloat16)
    d_grid, grad_grid_in, grad_grid_mix, grad_grid_out = branch_backward(upstream[:, :CH], grid_in, grid_mix, grid_out, grid_saved, grid_apply, grid_grad, factor)
    d_block, grad_block_in, grad_block_mix, grad_block_out = branch_backward(upstream[:, CH:], block_in, block_mix, block_out, block_saved, block_apply, block_grad, factor)
    first_d_hidden = (jnp.concatenate([d_grid, d_block], axis=-1) * gelu_slope(first_hidden)).astype(jnp.bfloat16)
    grad_w_in = gram_sum(first_normed, first_d_hidden) * factor
    feature_grad = (flat_cot.astype(jnp.float32) + normalize_back(matmul(first_d_hidden, w_in.T), first_unit, first_spread)).astype(jnp.bfloat16)
    return (result.reshape(H, W, CH), feature_grad.reshape(H, W, CH), grad_w_in, grad_grid_in, grad_grid_mix, grad_grid_out, grad_block_in, grad_block_mix, grad_block_out, grad_w_out)
```

```python
import math

import jax
import jax.numpy as jnp
from jax import lax
from jax.experimental import pallas as pl
from jax.experimental.pallas import tpu as pltpu
from jax.sharding import PartitionSpec as P

MESH = pl.DeviceIdType.MESH
F32 = jnp.float32
BF = jnp.bfloat16

ROWS, COLS, CH = 8, 16, 128
DEVS = ROWS * COLS
TILES = 8
TILE = 256
EARLY_A = 72
EARLY = 104
LATE = 40
LATE_AT = DEVS - LATE

epsilon = 1e-06
tanh_scale = 0.7978845608028654
cubic = 0.044715


def dot(left, right):
    return jnp.dot(left, right, preferred_element_type=F32)


def dot_nt(left, right):
    return lax.dot_general(left, right, (((1,), (1,)), ((), ())), preferred_element_type=F32)


def dot_tn(left, right):
    return lax.dot_general(left, right, (((0,), (0,)), ((), ())), preferred_element_type=F32)


def gelu_both(hidden):
    square = hidden * hidden
    inner = jnp.tanh(hidden * (tanh_scale + (tanh_scale * cubic) * square))
    half = 0.5 + 0.5 * inner
    value = hidden * half
    slope = half + value * (1.0 - half) * (2.0 * tanh_scale + (6.0 * tanh_scale * cubic) * square)
    return value, slope


def to_slots(values):
    pieces = []
    for group in range(16):
        pieces.append(values[group * 8 : group * 8 + 8])
        pieces.append(values[128 + group * 8 : 128 + group * 8 + 8])
    return jnp.concatenate(pieces, axis=0)


def from_slots(values):
    pieces = [values[group * 16 : group * 16 + 8] for group in range(16)]
    pieces += [values[group * 16 + 8 : group * 16 + 16] for group in range(16)]
    return jnp.concatenate(pieces, axis=0)


def kernel(
    feat, cot, w_in, grid_in, grid_mix, grid_out, block_in, block_mix, block_out, w_out,
    result, feature_grad, o_w_in, o_grid_in, o_grid_mix, o_grid_out, o_block_in, o_block_mix,
    o_block_out, o_w_out,
    sent, there, turned, back, x_mat, d_mat, x_mixed, d_mixed_back,
    n1_s, r1_s, slope1_s, z_s, n2_s, r2_s, slope2_s, gate_s, mix_s, mix_r_s, d_gated_s, up_s,
    joined_s, d_first_s,
    mean_mat, perm, perm_t, w_in_c, grid_in_c, block_in_c, grid_mix_t, block_mix_t,
    a_grid_in, a_grid_out, a_block_in, a_block_mix, a_block_out, a_w_in, a_w_out,
    early_out, early_in, early_all, late_out, late_in, late_all,
    send_sem, there_sem, back_sem, early_sem, early_all_sem, late_sem, late_all_sem,
):
    factor = 1.0 / math.sqrt(DEVS * TILES * TILE)
    r = lax.axis_index("row")
    c = lax.axis_index("col")
    me = r * COLS + c
    pair = c // 2
    my_slot = pair * 16 + r * 2 + lax.rem(c, 2)

    def peer_of(step):
        row = lax.rem(r + step // COLS, ROWS)
        col = lax.rem(c + lax.rem(step, COLS), COLS)
        return row, col

    barrier = pltpu.get_barrier_semaphore()

    def greet(step, carry):
        pl.semaphore_signal(barrier, inc=1, device_id=peer_of(step), device_id_type=MESH)
        return carry

    lax.fori_loop(1, DEVS, greet, 0)

    mean_mat[...] = jnp.full((CH, CH), 1.0 / CH, BF)

    def row_mean(values):
        return dot(values.astype(BF), mean_mat[...])

    def normalize(values_bf):
        values = values_bf.astype(F32)
        center = values - dot(values_bf, mean_mat[...])
        spread = lax.rsqrt(row_mean(center * center) + epsilon)
        return center * spread, spread

    def tile_of(ref, tile):
        at = pl.multiple_of(tile * 16, 16)
        return ref[:, pl.ds(at, 16), :].reshape(TILE, CH)

    def branch_pre(z_bf, upstream, in_weight, out_weight):
        unit, spread = normalize(z_bf)
        normed = unit.astype(BF)
        hidden = dot(normed, in_weight[...])
        gate, slope_gate = gelu_both(hidden[:, :CH])
        value, slope_mix = gelu_both(hidden[:, CH:])
        center = value - jnp.mean(value, axis=-1, keepdims=True)
        mix_spread = lax.rsqrt(row_mean(center * center) + epsilon)
        mix_input = center * mix_spread
        d_gated = dot_nt(upstream, out_weight[...])
        d_mixed = d_gated * gate
        return normed, spread, gate, slope_gate, slope_mix, mix_spread, mix_input, d_gated, d_mixed

    def branch_post(
        mixed, d_mix, z_bf, normed, spread, gate, slope_gate, slope_mix, mix_spread, mix_in,
        d_gated, upstream, in_centered, out_weight, acc_in, acc_out,
    ):
        mixed_one = mixed + 1.0
        gated = (gate * mixed_one).astype(BF)
        outcome = (z_bf.astype(F32) + dot(gated, out_weight[...])).astype(BF)
        acc_out[...] += dot_tn(gated, upstream)
        mix_unit = mix_in.astype(F32)
        d_value = mix_spread * (
            d_mix - row_mean(d_mix) - mix_unit * row_mean(d_mix * mix_unit)
        )
        d_hidden = jnp.concatenate(
            [(d_gated * mixed_one * slope_gate).astype(BF), (d_value * slope_mix).astype(BF)],
            axis=1,
        )
        acc_in[...] += dot_tn(normed, d_hidden)
        g = dot_nt(d_hidden, in_centered[...])
        unit = normed.astype(F32)
        d_branch = upstream.astype(F32) + spread * (g - unit * row_mean(g * unit))
        return outcome, d_branch

    def pre(step):
        tile = lax.rem(pair + step, TILES)
        x_bf = tile_of(feat, tile)
        unit, spread = normalize(x_bf)
        n1 = unit.astype(BF)
        n1_s[tile] = n1
        r1_s[tile] = spread
        value, slope = gelu_both(dot(n1, w_in[:, :CH]))
        slope1_s[tile] = slope
        z_bf = value.astype(BF)
        z_s[tile] = z_bf
        upstream = dot_nt(tile_of(cot, tile), w_out[:CH, :]).astype(BF)
        up_s[tile] = upstream
        normed, spread2, gate, slope_gate, slope_mix, mix_spread, mix_input, d_gated, d_mixed = (
            branch_pre(z_bf, upstream, grid_in, grid_out)
        )
        n2_s[tile] = normed
        r2_s[tile] = spread2
        gate_s[tile] = gate
        slope2_s[tile, :, :CH] = slope_gate
        slope2_s[tile, :, CH:] = slope_mix
        mix_r_s[tile] = mix_spread
        mix_s[tile] = mix_input.astype(BF)
        d_gated_s[tile] = d_gated
        slots = pl.ds(tile * 16, 16)
        sent[slots, 0:16, :] = to_slots(mix_input).astype(BF).reshape(16, 16, CH)
        sent[slots, 16:32, :] = to_slots(d_mixed).astype(BF).reshape(16, 16, CH)

    def send_there(step, first):
        tile = lax.rem(pair + step, TILES)

        def one(index, carry):
            row = lax.rem(r + index // 2, ROWS)
            side = lax.rem(c + index, 2)
            pltpu.make_async_remote_copy(
                src_ref=sent.at[tile * 16 + row * 2 + side],
                dst_ref=there.at[me],
                send_sem=send_sem.at[0],
                recv_sem=there_sem,
                device_id=(row, tile * 2 + side),
                device_id_type=MESH,
            ).start()
            return carry

        lax.fori_loop(first, 16, one, 0)

    pre(0)
    pl.semaphore_wait(barrier, DEVS - 1)
    pltpu.make_async_copy(sent.at[my_slot], there.at[me], there_sem).start()
    send_there(0, 1)

    def pre_step(step, carry):
        pre(step)
        send_there(step, 0)
        return carry

    lax.fori_loop(1, TILES, pre_step, 0)

    for ref, out in ((w_in, w_in_c), (grid_in, grid_in_c), (block_in, block_in_c)):
        weight = ref[...].astype(F32)
        out[...] = (weight - jnp.mean(weight, axis=0, keepdims=True)).astype(BF)
    at_row = lax.broadcasted_iota(jnp.int32, (TILE, TILE), 0)
    at_col = lax.broadcasted_iota(jnp.int32, (TILE, TILE), 1)
    eye = jnp.where(at_row == at_col, 1.0, 0.0).astype(BF)
    grid_mix_t[...] = dot_nt(eye, grid_mix[...]).astype(BF)
    block_mix_t[...] = dot_nt(eye, block_mix[...]).astype(BF)

    def place(index):
        return (index & 15) * 16 + ((index >> 4) & 1) * 8 + (index >> 5)

    perm[...] = jnp.where(at_col == place(at_row), 1.0, 0.0).astype(BF)
    perm_t[...] = jnp.where(at_row == place(at_col), 1.0, 0.0).astype(BF)
    for ref in (a_grid_in, a_grid_out, a_block_in, a_block_mix, a_block_out, a_w_in, a_w_out):
        ref[...] = jnp.zeros_like(ref)

    def block_step(tile, carry):
        n1 = n1_s[tile]
        cot_bf = tile_of(cot, tile)
        value, slope1 = gelu_both(dot(n1, w_in[:, CH:]))
        z_bf = value.astype(BF)
        upstream = dot_nt(cot_bf, w_out[CH:, :]).astype(BF)
        normed, spread, gate, slope_gate, slope_mix, mix_spread, mix_input, d_gated, d_mixed = (
            branch_pre(z_bf, upstream, block_in, block_out)
        )
        mix_in = mix_input.astype(BF)
        d_mixed = d_mixed.astype(BF)
        mixed = dot(block_mix[...], mix_in)
        d_mix = dot(block_mix_t[...], d_mixed)
        a_block_mix[...] += dot_nt(d_mixed, mix_in)
        outcome, d_branch = branch_post(
            mixed, d_mix, z_bf, normed, spread, gate, slope_gate, slope_mix, mix_spread, mix_in,
            d_gated, upstream, block_in_c, block_out, a_block_in, a_block_out,
        )
        joined_s[tile, :, CH:] = outcome
        a_w_out[CH:, :] += dot_tn(outcome, cot_bf)
        d_first = (d_branch * slope1).astype(BF)
        d_first_s[tile, :, CH:] = d_first
        a_w_in[:, CH:] += dot_tn(n1, d_first)
        return carry

    lax.fori_loop(0, TILES, block_step, 0)

    def pack(out, at, values):
        for left in range(0, values.shape[1], CH):
            count = values.shape[0] // 16
            piece = values[:, left : left + CH] * factor
            out[at : at + count] = piece.astype(BF).reshape(count, 16, CH)
            at += count
        return at

    def unpack(src, at, shape):
        halves = []
        for _ in range(0, shape[1], CH):
            count = shape[0] // 16
            halves.append(src[at : at + count].reshape(shape[0], CH).astype(F32))
            at += count
        return jnp.concatenate(halves, axis=1) if len(halves) > 1 else halves[0]

    at = pack(early_out, 0, a_block_in[...])
    at = pack(early_out, at, a_block_mix[...])
    at = pack(early_out, at, a_block_out[...])
    at = pack(early_out, at, a_w_out[CH:, :])
    pack(early_out, at, a_w_in[:, CH:])

    def scatter(out, into, least, most, shift, send, recv):
        def one(step, carry):
            row, col = peer_of(step)
            chunk = row * COLS + col - shift

            @pl.when((chunk >= least) & (chunk < most))
            def _():
                pltpu.make_async_remote_copy(
                    src_ref=out.at[chunk],
                    dst_ref=into.at[me],
                    send_sem=send,
                    recv_sem=recv,
                    device_id=(row, col),
                    device_id_type=MESH,
                ).start()

            return carry

        lax.fori_loop(1, DEVS, one, 0)

    def gather(buffer, chunk, send, recv):
        def one(step, carry):
            pltpu.make_async_remote_copy(
                src_ref=buffer.at[chunk],
                dst_ref=buffer.at[chunk],
                send_sem=send,
                recv_sem=recv,
                device_id=peer_of(step),
                device_id_type=MESH,
            ).start()
            return carry

        lax.fori_loop(1, DEVS, one, 0)

    def wait_for(sem, buffer, count):
        pltpu.make_async_copy(
            buffer.at[pl.ds(0, count)], buffer.at[pl.ds(0, count)], sem
        ).wait()

    scatter(early_out, early_in, 0, EARLY_A, 0, send_sem.at[2], early_sem)

    wait_for(there_sem, there, DEVS)

    def gather_positions(row, carry):
        source = pl.ds(row * 16, 16)
        at = pl.ds(pl.multiple_of(row * 32, 32), 32)
        for part, out in ((0, x_mat), (16, d_mat)):
            values = there[source, part : part + 16, :].reshape(TILE, CH)
            values = dot(perm[...], values).astype(BF)
            for offset in range(8):
                out[at, offset * CH : (offset + 1) * CH] = values[offset * 32 : offset * 32 + 32]
        return carry

    lax.fori_loop(0, ROWS, gather_positions, 0)
    x_mixed[...] = dot(grid_mix[...], x_mat[...]).astype(BF)
    d_mixed_back[...] = dot(grid_mix_t[...], d_mat[...]).astype(BF)

    def scatter_positions(row, carry):
        target = pl.ds(row * 16, 16)
        at = pl.ds(pl.multiple_of(row * 32, 32), 32)
        for part, src in ((0, x_mixed), (16, d_mixed_back)):
            values = jnp.concatenate(
                [src[at, offset * CH : (offset + 1) * CH] for offset in range(8)], axis=0
            )
            turned[target, part : part + 16, :] = (
                dot(perm_t[...], values).astype(BF).reshape(16, 16, CH)
            )
        return carry

    lax.fori_loop(0, ROWS, scatter_positions, 0)

    pltpu.make_async_copy(turned.at[me], back.at[my_slot], back_sem.at[pair]).start()

    def send_back(index, carry):
        tile = lax.rem(pair + index // 16, TILES)
        row = lax.rem(r + lax.rem(index, 16) // 2, ROWS)
        side = lax.rem(c + index, 2)
        col = tile * 2 + side
        pltpu.make_async_remote_copy(
            src_ref=turned.at[row * COLS + col],
            dst_ref=back.at[my_slot],
            send_sem=send_sem.at[1],
            recv_sem=back_sem.at[pair],
            device_id=(row, col),
            device_id_type=MESH,
        ).start()
        return carry

    lax.fori_loop(1, DEVS, send_back, 0)

    pack(early_out, EARLY_A, dot_nt(d_mat[...], x_mat[...]))
    scatter(early_out, early_in, EARLY_A, EARLY, 0, send_sem.at[2], early_sem)

    def reduce_chunk(out, into, every, chunk, send, recv, recv_all):
        into[me] = out[chunk]
        wait_for(recv, into, DEVS - 1)

        def add(index, total):
            return total + jnp.sum(into[pl.ds(index * 16, 16)].astype(F32), axis=0)

        total = lax.fori_loop(0, DEVS // 16, add, jnp.zeros((16, CH), F32))
        every[chunk] = total.astype(BF)
        gather(every, chunk, send, recv_all)

    @pl.when(me < EARLY)
    def _():
        reduce_chunk(
            early_out, early_in, early_all, me, send_sem.at[3], early_sem, early_all_sem
        )

    def grid_step(step, carry):
        tile = lax.rem(pair + TILES - step, TILES)
        wait_for(back_sem.at[tile], back, 16)
        slots = pl.ds(tile * 16, 16)
        mixed = from_slots(back[slots, 0:16, :].reshape(TILE, CH).astype(F32))
        d_mix = from_slots(back[slots, 16:32, :].reshape(TILE, CH).astype(F32))
        x_bf = tile_of(feat, tile)
        cot_bf = tile_of(cot, tile)
        n1 = n1_s[tile]
        outcome, d_branch = branch_post(
            mixed, d_mix, z_s[tile], n2_s[tile], r2_s[tile], gate_s[tile],
            slope2_s[tile, :, :CH], slope2_s[tile, :, CH:], mix_r_s[tile], mix_s[tile],
            d_gated_s[tile], up_s[tile], grid_in_c, grid_out, a_grid_in, a_grid_out,
        )
        joined = jnp.concatenate([outcome, joined_s[tile, :, CH:]], axis=1)
        a_w_out[:CH, :] += dot_tn(outcome, cot_bf)
        d_first = (d_branch * slope1_s[tile]).astype(BF)
        a_w_in[:, :CH] += dot_tn(n1, d_first)
        d_both = jnp.concatenate([d_first, d_first_s[tile, :, CH:]], axis=1)
        at = pl.ds(pl.multiple_of(tile * 16, 16), 16)
        out = (x_bf.astype(F32) + dot(joined, w_out[...])).astype(BF)
        result[:, at, :] = out.reshape(16, 16, CH)
        g = dot_nt(d_both, w_in_c[...])
        unit = n1.astype(F32)
        grad = cot_bf.astype(F32) + r1_s[tile] * (g - unit * row_mean(g * unit))
        feature_grad[:, at, :] = grad.astype(BF).reshape(16, 16, CH)
        return carry

    lax.fori_loop(0, TILES, grid_step, 0)

    at = pack(late_out, 0, a_grid_in[...])
    at = pack(late_out, at, a_grid_out[...])
    at = pack(late_out, at, a_w_out[:CH, :])
    pack(late_out, at, a_w_in[:, :CH])
    scatter(late_out, late_in, 0, LATE, LATE_AT, send_sem.at[4], late_sem)

    @pl.when(me >= LATE_AT)
    def _():
        reduce_chunk(
            late_out, late_in, late_all, me - LATE_AT, send_sem.at[5], late_sem, late_all_sem
        )

    @pl.when(me < EARLY)
    def _():
        wait_for(early_all_sem, early_all, EARLY - 1)
        wait_for(send_sem.at[2], early_out, EARLY - 1)

    @pl.when(me >= EARLY)
    def _():
        wait_for(early_all_sem, early_all, EARLY)
        wait_for(send_sem.at[2], early_out, EARLY)

    o_block_in[...] = unpack(early_all, 0, (128, 256))
    o_block_mix[...] = unpack(early_all, 16, (256, 256))
    o_block_out[...] = unpack(early_all, 48, (128, 128))
    o_w_out[CH:, :] = unpack(early_all, 56, (128, 128))
    o_w_in[:, CH:] = unpack(early_all, 64, (128, 128))
    o_grid_mix[...] = unpack(early_all, 72, (256, 256))

    wait_for(send_sem.at[0], sent, DEVS - 1)
    wait_for(send_sem.at[1], turned, DEVS - 1)

    @pl.when(me < EARLY)
    def _():
        wait_for(send_sem.at[3], early_in, DEVS - 1)

    @pl.when(me < LATE_AT)
    def _():
        wait_for(late_all_sem, late_all, LATE)
        wait_for(send_sem.at[4], late_out, LATE)

    @pl.when(me >= LATE_AT)
    def _():
        wait_for(late_all_sem, late_all, LATE - 1)
        wait_for(send_sem.at[4], late_out, LATE - 1)
        wait_for(send_sem.at[5], late_in, DEVS - 1)

    o_grid_in[...] = unpack(late_all, 0, (128, 256))
    o_grid_out[...] = unpack(late_all, 16, (128, 128))
    o_w_out[:CH, :] = unpack(late_all, 24, (128, 128))
    o_w_in[:, :CH] = unpack(late_all, 32, (128, 128))


def body(*args):
    def whole(dtype, *shape):
        return pltpu.VMEM(shape, dtype)

    pixels = (TILES, TILE, CH)
    both = (TILES, TILE, 2 * CH)
    scratch = [
        *[whole(BF, DEVS, 32, CH)] * 4,
        *[whole(BF, 256, 8 * CH)] * 4,
        whole(BF, *pixels),
        whole(F32, *pixels),
        whole(F32, *pixels),
        whole(BF, *pixels),
        whole(BF, *pixels),
        whole(F32, *pixels),
        whole(F32, *both),
        whole(F32, *pixels),
        whole(BF, *pixels),
        whole(F32, *pixels),
        whole(F32, *pixels),
        whole(BF, *pixels),
        whole(BF, *both),
        whole(BF, *both),
        whole(BF, CH, CH),
        *[whole(BF, TILE, TILE)] * 2,
        *[whole(BF, CH, 2 * CH)] * 3,
        *[whole(BF, 256, 256)] * 2,
        whole(F32, CH, 2 * CH),
        whole(F32, CH, CH),
        whole(F32, CH, 2 * CH),
        whole(F32, 256, 256),
        whole(F32, CH, CH),
        whole(F32, CH, 2 * CH),
        whole(F32, 2 * CH, CH),
        whole(BF, EARLY, 16, CH),
        whole(BF, DEVS, 16, CH),
        whole(BF, EARLY, 16, CH),
        whole(BF, LATE, 16, CH),
        whole(BF, DEVS, 16, CH),
        whole(BF, LATE, 16, CH),
        pltpu.SemaphoreType.DMA((6,)),
        pltpu.SemaphoreType.DMA,
        pltpu.SemaphoreType.DMA((TILES,)),
        *[pltpu.SemaphoreType.DMA] * 4,
    ]
    vmem = pl.BlockSpec(memory_space=pltpu.VMEM)
    shape = args[0].shape
    outs = [
        jax.ShapeDtypeStruct(shape, BF),
        jax.ShapeDtypeStruct(shape, BF),
        jax.ShapeDtypeStruct((128, 256), F32),
        jax.ShapeDtypeStruct((128, 256), F32),
        jax.ShapeDtypeStruct((256, 256), F32),
        jax.ShapeDtypeStruct((128, 128), F32),
        jax.ShapeDtypeStruct((128, 256), F32),
        jax.ShapeDtypeStruct((256, 256), F32),
        jax.ShapeDtypeStruct((128, 128), F32),
        jax.ShapeDtypeStruct((256, 128), F32),
    ]
    return tuple(
        pl.pallas_call(
            kernel,
            out_shape=outs,
            in_specs=[vmem] * 10,
            out_specs=[vmem] * 10,
            scratch_shapes=scratch,
            compiler_params=pltpu.CompilerParams(
                collective_id=0, has_side_effects=True, vmem_limit_bytes=56 * 2**20
            ),
        )(*args)
    )


def solution(mesh):
    split = P("row", "col", None)
    return jax.shard_map(
        body,
        mesh=mesh,
        in_specs=(split, split) + (P(),) * 8,
        out_specs=(split, split) + (P(),) * 8,
        check_vma=False,
    )
```

```python
import math

import jax
import jax.numpy as jnp
from jax import lax
from jax.experimental import pallas as pl
from jax.experimental.pallas import tpu as pltpu
from jax.sharding import PartitionSpec as P

MESH = pl.DeviceIdType.MESH
F32 = jnp.float32
BF = jnp.bfloat16

ROWS, COLS, CH = 8, 16, 128
DEVS = ROWS * COLS
TILES = 8
TILE = 256
EARLY_A = 72
EARLY = 104
LATE = 40
SPREAD = 3
UNSPREAD = 43
PRE_FIRST = 4

epsilon = 1e-06
tanh_scale = 0.7978845608028654
cubic = 0.044715


def dot(left, right):
    return jnp.dot(left, right, preferred_element_type=F32)


def dot_nt(left, right):
    return lax.dot_general(left, right, (((1,), (1,)), ((), ())), preferred_element_type=F32)


def dot_tn(left, right):
    return lax.dot_general(left, right, (((0,), (0,)), ((), ())), preferred_element_type=F32)


def gelu_both(hidden):
    square = hidden * hidden
    inner = jnp.tanh(hidden * (tanh_scale + (tanh_scale * cubic) * square))
    half = 0.5 + 0.5 * inner
    value = hidden * half
    slope = half + value * (1.0 - half) * (2.0 * tanh_scale + (6.0 * tanh_scale * cubic) * square)
    return value, slope


def to_slots(values):
    pieces = []
    for group in range(16):
        pieces.append(values[group * 8 : group * 8 + 8])
        pieces.append(values[128 + group * 8 : 128 + group * 8 + 8])
    return jnp.concatenate(pieces, axis=0)


def from_slots(values):
    pieces = [values[group * 16 : group * 16 + 8] for group in range(16)]
    pieces += [values[group * 16 + 8 : group * 16 + 16] for group in range(16)]
    return jnp.concatenate(pieces, axis=0)


def kernel(
    feat_hbm, cot_hbm, w_in, grid_in, grid_mix, grid_out, block_in, block_mix, block_out, w_out,
    result, feature_grad, early_res, late_res,
    feat, cot, result_v, feature_grad_v, sent, there, turned, back, x_mat, d_mat, x_mixed, d_mixed_back,
    n1_s, r1_s, slope1_s, z_s, n2_s, r2_s, slope2_s, gate_s, mix_s, mix_r_s, d_gated_s, up_s,
    joined_s, d_first_s,
    perm, perm_t, w_in_ct, grid_in_ct, block_in_ct, grid_mix_t, block_mix_t, w_out_t, grid_out_t,
    block_out_t,
    a_grid_in, a_grid_out, a_block_in, a_block_mix, a_block_out, a_w_in, a_w_out,
    early_out, early_in, early_all, late_out, late_in, late_all,
    send_sem, there_sem, back_sem, early_sem, early_all_sem, late_sem, late_all_sem, io_sem,
):
    factor = 1.0 / math.sqrt(DEVS * TILES * TILE)
    r = lax.axis_index("row")
    c = lax.axis_index("col")
    me = r * COLS + c
    mine = lax.rem(me * UNSPREAD, DEVS)
    pair = c // 2
    my_slot = pair * 16 + r * 2 + lax.rem(c, 2)

    def peer_of(step):
        row = lax.rem(r + step // COLS, ROWS)
        col = lax.rem(c + lax.rem(step, COLS), COLS)
        return row, col

    feat_in = pltpu.make_async_copy(feat_hbm, feat, io_sem.at[0])
    cot_in = pltpu.make_async_copy(cot_hbm, cot, io_sem.at[1])
    feat_in.start()
    cot_in.start()

    barrier = pltpu.get_barrier_semaphore()

    def greet(step, carry):
        pl.semaphore_signal(barrier, inc=1, device_id=peer_of(step), device_id_type=MESH)
        return carry

    lax.fori_loop(1, DEVS, greet, 0)

    def row_mean(values):
        return jnp.mean(values, axis=-1, keepdims=True)

    def normalize(values_bf):
        values = values_bf.astype(F32)
        center = values - row_mean(values)
        spread = lax.rsqrt(row_mean(center * center) + epsilon)
        return center * spread, spread

    def tile_of(ref, tile):
        at = pl.multiple_of(tile * 16, 16)
        return ref[:, pl.ds(at, 16), :].reshape(TILE, CH)

    def branch_pre(z_bf, upstream, in_weight, out_weight_t):
        unit, spread = normalize(z_bf)
        normed = unit.astype(BF)
        hidden = dot(normed, in_weight[...])
        gate, slope_gate = gelu_both(hidden[:, :CH])
        value, slope_mix = gelu_both(hidden[:, CH:])
        center = value - row_mean(value)
        mix_spread = lax.rsqrt(row_mean(center * center) + epsilon)
        mix_input = center * mix_spread
        d_gated = dot(upstream, out_weight_t[...])
        d_mixed = d_gated * gate
        return normed, spread, gate, slope_gate, slope_mix, mix_spread, mix_input, d_gated, d_mixed

    def branch_post(
        mixed, d_mix, z_bf, normed, spread, gate, slope_gate, slope_mix, mix_spread, mix_in,
        d_gated, upstream, in_centered_t, out_weight, acc_in, acc_out,
    ):
        mixed_one = mixed + 1.0
        gated = (gate * mixed_one).astype(BF)
        outcome = (z_bf.astype(F32) + dot(gated, out_weight[...])).astype(BF)
        acc_out[...] += dot_tn(gated, upstream)
        mix_unit = mix_in.astype(F32)
        d_value = mix_spread * (
            d_mix - row_mean(d_mix) - mix_unit * row_mean(d_mix * mix_unit)
        )
        d_hidden = jnp.concatenate(
            [(d_gated * mixed_one * slope_gate).astype(BF), (d_value * slope_mix).astype(BF)],
            axis=1,
        )
        acc_in[...] += dot_tn(normed, d_hidden)
        g = dot(d_hidden, in_centered_t[...])
        unit = normed.astype(F32)
        d_branch = upstream.astype(F32) + spread * (g - unit * row_mean(g * unit))
        return outcome, d_branch

    def pre(step):
        tile = lax.rem(pair + step, TILES)
        x_bf = tile_of(feat, tile)
        unit, spread = normalize(x_bf)
        n1 = unit.astype(BF)
        n1_s[tile] = n1
        r1_s[tile] = jnp.broadcast_to(spread, (TILE, CH))
        value, slope = gelu_both(dot(n1, w_in[:, :CH]))
        slope1_s[tile] = slope
        z_bf = value.astype(BF)
        z_s[tile] = z_bf
        upstream = dot(tile_of(cot, tile), w_out_t[:, :CH]).astype(BF)
        up_s[tile] = upstream
        normed, spread2, gate, slope_gate, slope_mix, mix_spread, mix_input, d_gated, d_mixed = (
            branch_pre(z_bf, upstream, grid_in, grid_out_t)
        )
        n2_s[tile] = normed
        r2_s[tile] = jnp.broadcast_to(spread2, (TILE, CH))
        gate_s[tile] = gate
        slope2_s[tile, :, :CH] = slope_gate
        slope2_s[tile, :, CH:] = slope_mix
        mix_r_s[tile] = jnp.broadcast_to(mix_spread, (TILE, CH))
        mix_s[tile] = mix_input.astype(BF)
        d_gated_s[tile] = d_gated
        slots = pl.ds(tile * 16, 16)
        sent[slots, 0:16, :] = to_slots(mix_input).astype(BF).reshape(16, 16, CH)
        sent[slots, 16:32, :] = to_slots(d_mixed).astype(BF).reshape(16, 16, CH)

    def send_there(step, first):
        tile = lax.rem(pair + step, TILES)

        def one(index, carry):
            row = lax.rem(r + index // 2, ROWS)
            side = lax.rem(c + index, 2)
            pltpu.make_async_remote_copy(
                src_ref=sent.at[tile * 16 + row * 2 + side],
                dst_ref=there.at[me],
                send_sem=send_sem.at[0],
                recv_sem=there_sem,
                device_id=(row, tile * 2 + side),
                device_id_type=MESH,
            ).start()
            return carry

        lax.fori_loop(first, 16, one, 0)

    at_row = lax.broadcasted_iota(jnp.int32, (TILE, TILE), 0)
    at_col = lax.broadcasted_iota(jnp.int32, (TILE, TILE), 1)
    eye = jnp.where(at_row == at_col, 1.0, 0.0).astype(BF)
    eye_half = eye[:CH, :CH]
    w_out_t[...] = dot_nt(eye_half, w_out[...]).astype(BF)
    grid_out_t[...] = dot_nt(eye_half, grid_out[...]).astype(BF)

    def prepare():
        block_out_t[...] = dot_nt(eye_half, block_out[...]).astype(BF)
        for ref, out in ((w_in, w_in_ct), (grid_in, grid_in_ct), (block_in, block_in_ct)):
            weight = ref[...].astype(F32)
            centered = (weight - jnp.mean(weight, axis=0, keepdims=True)).astype(BF)
            out[...] = dot_nt(eye, centered).astype(BF)
        grid_mix_t[...] = dot_nt(eye, grid_mix[...]).astype(BF)
        block_mix_t[...] = dot_nt(eye, block_mix[...]).astype(BF)

        def place(index):
            return (index & 15) * 16 + ((index >> 4) & 1) * 8 + (index >> 5)

        perm[...] = jnp.where(at_col == place(at_row), 1.0, 0.0).astype(BF)
        perm_t[...] = jnp.where(at_row == place(at_col), 1.0, 0.0).astype(BF)
        for ref in (a_grid_in, a_grid_out, a_block_in, a_block_mix, a_block_out, a_w_in, a_w_out):
            ref[...] = jnp.zeros_like(ref)

    feat_in.wait()
    cot_in.wait()
    prepare()
    lax.fori_loop(0, PRE_FIRST, lambda step, carry: (pre(step), carry)[1], 0)
    pl.semaphore_wait(barrier, DEVS - 1)
    pltpu.make_async_copy(sent.at[my_slot], there.at[me], there_sem).start()
    send_there(0, 1)
    lax.fori_loop(1, PRE_FIRST, lambda step, carry: (send_there(step, 0), carry)[1], 0)

    def pre_step(step, carry):
        pre(step)
        send_there(step, 0)
        return carry

    lax.fori_loop(PRE_FIRST, TILES, pre_step, 0)

    def block_step(tile, carry):
        n1 = n1_s[tile]
        cot_bf = tile_of(cot, tile)
        value, slope1 = gelu_both(dot(n1, w_in[:, CH:]))
        z_bf = value.astype(BF)
        upstream = dot(cot_bf, w_out_t[:, CH:]).astype(BF)
        normed, spread, gate, slope_gate, slope_mix, mix_spread, mix_input, d_gated, d_mixed = (
            branch_pre(z_bf, upstream, block_in, block_out_t)
        )
        mix_in = mix_input.astype(BF)
        d_mixed = d_mixed.astype(BF)
        mixed = dot(block_mix[...], mix_in)
        d_mix = dot(block_mix_t[...], d_mixed)
        a_block_mix[...] += dot_nt(d_mixed, mix_in)
        outcome, d_branch = branch_post(
            mixed, d_mix, z_bf, normed, spread, gate, slope_gate, slope_mix, mix_spread, mix_in,
            d_gated, upstream, block_in_ct, block_out, a_block_in, a_block_out,
        )
        joined_s[tile, :, CH:] = outcome
        a_w_out[CH:, :] += dot_tn(outcome, cot_bf)
        d_first = (d_branch * slope1).astype(BF)
        d_first_s[tile, :, CH:] = d_first
        a_w_in[:, CH:] += dot_tn(n1, d_first)
        return carry

    def block_pair(index, carry):
        block_step(index * 2, 0)
        block_step(index * 2 + 1, 0)
        return carry

    lax.fori_loop(0, TILES // 2, block_pair, 0)

    def pack(out, at, values):
        for left in range(0, values.shape[1], CH):
            count = values.shape[0] // 16
            piece = values[:, left : left + CH] * factor
            out[at : at + count] = piece.astype(BF).reshape(count, 16, CH)
            at += count
        return at

    def scatter(out, into, least, most, send, recv):
        def one(index, carry):
            chunk = least + lax.rem(index + me, most - least)
            to = lax.rem(chunk * SPREAD, DEVS)

            @pl.when(to != me)
            def _():
                pltpu.make_async_remote_copy(
                    src_ref=out.at[chunk],
                    dst_ref=into.at[me],
                    send_sem=send,
                    recv_sem=recv,
                    device_id=(to // COLS, lax.rem(to, COLS)),
                    device_id_type=MESH,
                ).start()

            return carry

        lax.fori_loop(0, most - least, one, 0)

    def gather(buffer, chunk, send, recv):
        def one(step, carry):
            pltpu.make_async_remote_copy(
                src_ref=buffer.at[chunk],
                dst_ref=buffer.at[chunk],
                send_sem=send,
                recv_sem=recv,
                device_id=peer_of(step),
                device_id_type=MESH,
            ).start()
            return carry

        lax.fori_loop(1, DEVS, one, 0)

    def wait_for(sem, buffer, count):
        pltpu.make_async_copy(
            buffer.at[pl.ds(0, count)], buffer.at[pl.ds(0, count)], sem
        ).wait()

    at = pack(early_out, 0, a_block_in[...])
    at = pack(early_out, at, a_block_mix[...])
    at = pack(early_out, at, a_block_out[...])
    at = pack(early_out, at, a_w_out[CH:, :])
    pack(early_out, at, a_w_in[:, CH:])
    scatter(early_out, early_in, 0, EARLY_A, send_sem.at[2], early_sem)

    wait_for(there_sem, there, DEVS)

    def gather_positions(row, carry):
        source = pl.ds(row * 16, 16)
        at = pl.ds(pl.multiple_of(row * 32, 32), 32)
        for part, out in ((0, x_mat), (16, d_mat)):
            values = there[source, part : part + 16, :].reshape(TILE, CH)
            values = dot(perm[...], values).astype(BF)
            for offset in range(8):
                out[at, offset * CH : (offset + 1) * CH] = values[offset * 32 : offset * 32 + 32]
        return carry

    lax.fori_loop(0, ROWS, gather_positions, 0)
    pack(early_out, EARLY_A, dot_nt(d_mat[...], x_mat[...]))
    scatter(early_out, early_in, EARLY_A, EARLY, send_sem.at[2], early_sem)
    x_mixed[...] = dot(grid_mix[...], x_mat[...]).astype(BF)
    d_mixed_back[...] = dot(grid_mix_t[...], d_mat[...]).astype(BF)

    def scatter_positions(row, carry):
        target = pl.ds(row * 16, 16)
        at = pl.ds(pl.multiple_of(row * 32, 32), 32)
        for part, src in ((0, x_mixed), (16, d_mixed_back)):
            values = jnp.concatenate(
                [src[at, offset * CH : (offset + 1) * CH] for offset in range(8)], axis=0
            )
            turned[target, part : part + 16, :] = (
                dot(perm_t[...], values).astype(BF).reshape(16, 16, CH)
            )
        return carry

    lax.fori_loop(0, ROWS, scatter_positions, 0)

    pltpu.make_async_copy(turned.at[me], back.at[my_slot], back_sem.at[pair]).start()

    def send_back(index, carry):
        tile = lax.rem(pair + index // 16, TILES)
        row = lax.rem(r + lax.rem(index, 16) // 2, ROWS)
        side = lax.rem(c + index, 2)
        col = tile * 2 + side
        pltpu.make_async_remote_copy(
            src_ref=turned.at[row * COLS + col],
            dst_ref=back.at[my_slot],
            send_sem=send_sem.at[1],
            recv_sem=back_sem.at[pair],
            device_id=(row, col),
            device_id_type=MESH,
        ).start()
        return carry

    lax.fori_loop(1, DEVS, send_back, 0)

    def reduce_chunk(out, into, every, chunk, send, recv, recv_all):
        into[me] = out[chunk]
        wait_for(recv, into, DEVS - 1)

        def add(index, total):
            return total + jnp.sum(into[pl.ds(index * 16, 16)].astype(F32), axis=0)

        total = lax.fori_loop(0, DEVS // 16, add, jnp.zeros((16, CH), F32))
        every[chunk] = total.astype(BF)
        gather(every, chunk, send, recv_all)

    @pl.when(mine < EARLY)
    def _():
        reduce_chunk(
            early_out, early_in, early_all, mine, send_sem.at[3], early_sem, early_all_sem
        )

    def grid_step(step, carry):
        tile = lax.rem(pair + TILES - step, TILES)
        wait_for(back_sem.at[tile], back, 16)
        slots = pl.ds(tile * 16, 16)
        mixed = from_slots(back[slots, 0:16, :].reshape(TILE, CH).astype(F32))
        d_mix = from_slots(back[slots, 16:32, :].reshape(TILE, CH).astype(F32))
        x_bf = tile_of(feat, tile)
        cot_bf = tile_of(cot, tile)
        n1 = n1_s[tile]
        outcome, d_branch = branch_post(
            mixed, d_mix, z_s[tile], n2_s[tile], r2_s[tile], gate_s[tile],
            slope2_s[tile, :, :CH], slope2_s[tile, :, CH:], mix_r_s[tile], mix_s[tile],
            d_gated_s[tile], up_s[tile], grid_in_ct, grid_out, a_grid_in, a_grid_out,
        )
        joined = jnp.concatenate([outcome, joined_s[tile, :, CH:]], axis=1)
        a_w_out[:CH, :] += dot_tn(outcome, cot_bf)
        d_first = (d_branch * slope1_s[tile]).astype(BF)
        a_w_in[:, :CH] += dot_tn(n1, d_first)
        d_both = jnp.concatenate([d_first, d_first_s[tile, :, CH:]], axis=1)
        at = pl.ds(pl.multiple_of(tile * 16, 16), 16)
        out = (x_bf.astype(F32) + dot(joined, w_out[...])).astype(BF)
        result_v[:, at, :] = out.reshape(16, 16, CH)
        g = dot(d_both, w_in_ct[...])
        unit = n1.astype(F32)
        grad = cot_bf.astype(F32) + r1_s[tile] * (g - unit * row_mean(g * unit))
        feature_grad_v[:, at, :] = grad.astype(BF).reshape(16, 16, CH)
        return carry

    lax.fori_loop(0, TILES, grid_step, 0)
    result_out = pltpu.make_async_copy(result_v, result, io_sem.at[2])
    feature_grad_out = pltpu.make_async_copy(feature_grad_v, feature_grad, io_sem.at[3])
    result_out.start()
    feature_grad_out.start()

    at = pack(late_out, 0, a_grid_in[...])
    at = pack(late_out, at, a_grid_out[...])
    at = pack(late_out, at, a_w_out[:CH, :])
    pack(late_out, at, a_w_in[:, :CH])
    scatter(late_out, late_in, 0, LATE, send_sem.at[4], late_sem)

    @pl.when(mine < LATE)
    def _():
        reduce_chunk(
            late_out, late_in, late_all, mine, send_sem.at[5], late_sem, late_all_sem
        )

    @pl.when(mine < EARLY)
    def _():
        wait_for(early_all_sem, early_all, EARLY - 1)
        wait_for(send_sem.at[2], early_out, EARLY - 1)

    @pl.when(mine >= EARLY)
    def _():
        wait_for(early_all_sem, early_all, EARLY)
        wait_for(send_sem.at[2], early_out, EARLY)

    wait_for(send_sem.at[0], sent, DEVS - 1)
    wait_for(send_sem.at[1], turned, DEVS - 1)

    @pl.when(mine < EARLY)
    def _():
        wait_for(send_sem.at[3], early_in, DEVS - 1)

    @pl.when(mine >= LATE)
    def _():
        wait_for(late_all_sem, late_all, LATE)
        wait_for(send_sem.at[4], late_out, LATE)

    @pl.when(mine < LATE)
    def _():
        wait_for(late_all_sem, late_all, LATE - 1)
        wait_for(send_sem.at[4], late_out, LATE - 1)
        wait_for(send_sem.at[5], late_in, DEVS - 1)

    early_res[...] = early_all[...]
    late_res[...] = late_all[...]
    result_out.wait()
    feature_grad_out.wait()


def unpack(src, at, shape):
    halves = []
    for _ in range(0, shape[1], CH):
        count = shape[0] // 16
        halves.append(src[at : at + count].reshape(shape[0], CH).astype(F32))
        at += count
    return jnp.concatenate(halves, axis=1) if len(halves) > 1 else halves[0]


def finish(
    result_in, feature_grad_in, early_all, late_all,
    result, feature_grad, o_w_in, o_grid_in, o_grid_mix, o_grid_out, o_block_in, o_block_mix,
    o_block_out, o_w_out, sem,
):
    copies = [
        pltpu.make_async_copy(result_in, result, sem.at[0]),
        pltpu.make_async_copy(feature_grad_in, feature_grad, sem.at[1]),
    ]
    for copy in copies:
        copy.start()
    o_block_in[...] = unpack(early_all, 0, (128, 256))
    o_block_mix[...] = unpack(early_all, 16, (256, 256))
    o_block_out[...] = unpack(early_all, 48, (128, 128))
    o_w_out[CH:, :] = unpack(early_all, 56, (128, 128))
    o_w_in[:, CH:] = unpack(early_all, 64, (128, 128))
    o_grid_mix[...] = unpack(early_all, 72, (256, 256))
    o_grid_in[...] = unpack(late_all, 0, (128, 256))
    o_grid_out[...] = unpack(late_all, 16, (128, 128))
    o_w_out[:CH, :] = unpack(late_all, 24, (128, 128))
    o_w_in[:, :CH] = unpack(late_all, 32, (128, 128))
    for copy in copies:
        copy.wait()


def body(*args):
    def whole(dtype, *shape):
        return pltpu.VMEM(shape, dtype)

    pixels = (TILES, TILE, CH)
    both = (TILES, TILE, 2 * CH)
    scratch = [
        *[whole(BF, 16, 128, CH)] * 4,
        *[whole(BF, DEVS, 32, CH)] * 4,
        *[whole(BF, 256, 8 * CH)] * 4,
        whole(BF, *pixels),
        whole(F32, *pixels),
        whole(F32, *pixels),
        whole(BF, *pixels),
        whole(BF, *pixels),
        whole(F32, *pixels),
        whole(F32, *both),
        whole(F32, *pixels),
        whole(BF, *pixels),
        whole(F32, *pixels),
        whole(F32, *pixels),
        whole(BF, *pixels),
        whole(BF, *both),
        whole(BF, *both),
        *[whole(BF, TILE, TILE)] * 2,
        *[whole(BF, 2 * CH, CH)] * 3,
        *[whole(BF, 256, 256)] * 2,
        whole(BF, CH, 2 * CH),
        *[whole(BF, CH, CH)] * 2,
        whole(F32, CH, 2 * CH),
        whole(F32, CH, CH),
        whole(F32, CH, 2 * CH),
        whole(F32, 256, 256),
        whole(F32, CH, CH),
        whole(F32, CH, 2 * CH),
        whole(F32, 2 * CH, CH),
        whole(BF, EARLY, 16, CH),
        whole(BF, DEVS, 16, CH),
        whole(BF, EARLY, 16, CH),
        whole(BF, LATE, 16, CH),
        whole(BF, DEVS, 16, CH),
        whole(BF, LATE, 16, CH),
        pltpu.SemaphoreType.DMA((6,)),
        pltpu.SemaphoreType.DMA,
        pltpu.SemaphoreType.DMA((TILES,)),
        *[pltpu.SemaphoreType.DMA] * 4,
        pltpu.SemaphoreType.DMA((4,)),
    ]
    vmem = pl.BlockSpec(memory_space=pltpu.VMEM)
    shape = args[0].shape
    outs = [
        jax.ShapeDtypeStruct(shape, BF),
        jax.ShapeDtypeStruct(shape, BF),
        jax.ShapeDtypeStruct((128, 256), F32),
        jax.ShapeDtypeStruct((128, 256), F32),
        jax.ShapeDtypeStruct((256, 256), F32),
        jax.ShapeDtypeStruct((128, 128), F32),
        jax.ShapeDtypeStruct((128, 256), F32),
        jax.ShapeDtypeStruct((256, 256), F32),
        jax.ShapeDtypeStruct((128, 128), F32),
        jax.ShapeDtypeStruct((256, 128), F32),
    ]
    hbm = pl.BlockSpec(memory_space=pl.ANY)
    parts = pl.pallas_call(
        kernel,
        out_shape=[
            outs[0],
            outs[1],
            jax.ShapeDtypeStruct((EARLY, 16, CH), BF),
            jax.ShapeDtypeStruct((LATE, 16, CH), BF),
        ],
        in_specs=[hbm] * 2 + [vmem] * 8,
        out_specs=[hbm] * 2 + [vmem] * 2,
        scratch_shapes=scratch,
        compiler_params=pltpu.CompilerParams(
            collective_id=0, has_side_effects=True, vmem_limit_bytes=56 * 2**20
        ),
    )(*args)
    return tuple(
        pl.pallas_call(
            finish,
            out_shape=outs,
            in_specs=[vmem] * 4,
            out_specs=[hbm] * 2 + [vmem] * 8,
            scratch_shapes=[pltpu.SemaphoreType.DMA((2,))],
        )(*parts)
    )


def solution(mesh):
    split = P("row", "col", None)
    return jax.shard_map(
        body,
        mesh=mesh,
        in_specs=(split, split) + (P(),) * 8,
        out_specs=(split, split) + (P(),) * 8,
        check_vma=False,
    )
```

```python
import math

import jax
import jax.numpy as jnp
from jax import lax
from jax.experimental import pallas as pl
from jax.experimental.pallas import tpu as pltpu
from jax.sharding import PartitionSpec as P

MESH = pl.DeviceIdType.MESH
F32 = jnp.float32
BF = jnp.bfloat16

ROWS, COLS, CH = 8, 16, 128
DEVS = ROWS * COLS
TILES = 8
TILE = 256
EARLY_A = 72
EARLY = 104
LATE = 40
SPREAD = 3
UNSPREAD = 43
PRE_FIRST = 4

epsilon = 1e-06
tanh_scale = 0.7978845608028654
cubic = 0.044715


def dot(left, right):
    return jnp.dot(left, right, preferred_element_type=F32)


def dot_nt(left, right):
    return lax.dot_general(left, right, (((1,), (1,)), ((), ())), preferred_element_type=F32)


def dot_tn(left, right):
    return lax.dot_general(left, right, (((0,), (0,)), ((), ())), preferred_element_type=F32)


def gelu_both(hidden):
    square = hidden * hidden
    inner = jnp.tanh(hidden * (tanh_scale + (tanh_scale * cubic) * square))
    half = 0.5 + 0.5 * inner
    value = hidden * half
    slope = half + value * (1.0 - half) * (2.0 * tanh_scale + (6.0 * tanh_scale * cubic) * square)
    return value, slope


def to_slots(values):
    pieces = []
    for group in range(16):
        pieces.append(values[group * 8 : group * 8 + 8])
        pieces.append(values[128 + group * 8 : 128 + group * 8 + 8])
    return jnp.concatenate(pieces, axis=0)


def from_slots(values):
    pieces = [values[group * 16 : group * 16 + 8] for group in range(16)]
    pieces += [values[group * 16 + 8 : group * 16 + 16] for group in range(16)]
    return jnp.concatenate(pieces, axis=0)


def kernel(
    feat_hbm, cot_hbm, w_in, grid_in, grid_mix, grid_out, block_in, block_mix, block_out, w_out,
    result, feature_grad, early_res, late_res,
    feat, cot, result_v, feature_grad_v, sent, there, turned, back, x_mat, d_mat, x_mixed, d_mixed_back,
    n1_s, r1_s, slope1_s, z_s, n2_s, r2_s, slope2_s, gate_s, mix_s, mix_r_s, d_gated_s, up_s,
    joined_s, d_first_s,
    perm, perm_t, w_in_ct, grid_in_ct, block_in_ct, grid_mix_t, block_mix_t, w_out_t, grid_out_t,
    block_out_t,
    a_grid_in, a_grid_out, a_block_in, a_block_mix, a_block_out, a_w_in, a_w_out,
    early_out, early_in, early_all, late_out, late_in, late_all,
    send_sem, there_sem, back_sem, early_sem, early_all_sem, late_sem, late_all_sem, io_sem,
):
    factor = 1.0 / math.sqrt(DEVS * TILES * TILE)
    r = lax.axis_index("row")
    c = lax.axis_index("col")
    me = r * COLS + c
    mine = lax.rem(me * UNSPREAD, DEVS)
    pair = c // 2
    my_slot = pair * 16 + r * 2 + lax.rem(c, 2)

    def peer_of(step):
        row = lax.rem(r + step // COLS, ROWS)
        col = lax.rem(c + lax.rem(step, COLS), COLS)
        return row, col

    feat_in = pltpu.make_async_copy(feat_hbm, feat, io_sem.at[0])
    cot_in = pltpu.make_async_copy(cot_hbm, cot, io_sem.at[1])
    feat_in.start()
    cot_in.start()

    barrier = pltpu.get_barrier_semaphore()

    def greet(step, carry):
        pl.semaphore_signal(barrier, inc=1, device_id=peer_of(step), device_id_type=MESH)
        return carry

    lax.fori_loop(1, DEVS, greet, 0)

    def row_mean(values):
        return jnp.mean(values, axis=-1, keepdims=True)

    def normalize(values_bf):
        values = values_bf.astype(F32)
        center = values - row_mean(values)
        spread = lax.rsqrt(row_mean(center * center) + epsilon)
        return center * spread, spread

    def tile_of(ref, tile):
        at = pl.multiple_of(tile * 16, 16)
        return ref[:, pl.ds(at, 16), :].reshape(TILE, CH)

    def branch_pre(z_bf, upstream, in_weight, out_weight_t):
        unit, spread = normalize(z_bf)
        normed = unit.astype(BF)
        hidden = dot(normed, in_weight[...])
        gate, slope_gate = gelu_both(hidden[:, :CH])
        value, slope_mix = gelu_both(hidden[:, CH:])
        center = value - row_mean(value)
        mix_spread = lax.rsqrt(row_mean(center * center) + epsilon)
        mix_input = center * mix_spread
        d_gated = dot(upstream, out_weight_t[...])
        d_mixed = d_gated * gate
        return normed, spread, gate, slope_gate, slope_mix, mix_spread, mix_input, d_gated, d_mixed

    def branch_post(
        mixed, d_mix, z_bf, normed, spread, gate, slope_gate, slope_mix, mix_spread, mix_in,
        d_gated, upstream, in_centered_t, out_weight, acc_in, acc_out,
    ):
        mixed_one = mixed + 1.0
        gated = (gate * mixed_one).astype(BF)
        outcome = (z_bf.astype(F32) + dot(gated, out_weight[...])).astype(BF)
        acc_out[...] += dot_tn(gated, upstream)
        mix_unit = mix_in.astype(F32)
        d_value = mix_spread * (
            d_mix - row_mean(d_mix) - mix_unit * row_mean(d_mix * mix_unit)
        )
        d_hidden = jnp.concatenate(
            [(d_gated * mixed_one * slope_gate).astype(BF), (d_value * slope_mix).astype(BF)],
            axis=1,
        )
        acc_in[...] += dot_tn(normed, d_hidden)
        g = dot(d_hidden, in_centered_t[...])
        unit = normed.astype(F32)
        d_branch = upstream.astype(F32) + spread * (g - unit * row_mean(g * unit))
        return outcome, d_branch

    def pre(step):
        tile = lax.rem(pair + step, TILES)
        x_bf = tile_of(feat, tile)
        unit, spread = normalize(x_bf)
        n1 = unit.astype(BF)
        n1_s[tile] = n1
        r1_s[tile] = jnp.broadcast_to(spread, (TILE, CH))
        value, slope = gelu_both(dot(n1, w_in[:, :CH]))
        slope1_s[tile] = slope
        z_bf = value.astype(BF)
        z_s[tile] = z_bf
        upstream = dot(tile_of(cot, tile), w_out_t[:, :CH]).astype(BF)
        up_s[tile] = upstream
        normed, spread2, gate, slope_gate, slope_mix, mix_spread, mix_input, d_gated, d_mixed = (
            branch_pre(z_bf, upstream, grid_in, grid_out_t)
        )
        n2_s[tile] = normed
        r2_s[tile] = jnp.broadcast_to(spread2, (TILE, CH))
        gate_s[tile] = gate
        slope2_s[tile, :, :CH] = slope_gate
        slope2_s[tile, :, CH:] = slope_mix
        mix_r_s[tile] = jnp.broadcast_to(mix_spread, (TILE, CH))
        mix_s[tile] = mix_input.astype(BF)
        d_gated_s[tile] = d_gated
        slots = pl.ds(tile * 16, 16)
        sent[slots, 0:16, :] = to_slots(mix_input).astype(BF).reshape(16, 16, CH)
        sent[slots, 16:32, :] = to_slots(d_mixed).astype(BF).reshape(16, 16, CH)

    def send_there(step, first):
        tile = lax.rem(pair + step, TILES)

        def one(index, carry):
            row = lax.rem(r + index // 2, ROWS)
            side = lax.rem(c + index, 2)
            pltpu.make_async_remote_copy(
                src_ref=sent.at[tile * 16 + row * 2 + side],
                dst_ref=there.at[me],
                send_sem=send_sem.at[0],
                recv_sem=there_sem,
                device_id=(row, tile * 2 + side),
                device_id_type=MESH,
            ).start()
            return carry

        lax.fori_loop(first, 16, one, 0)

    at_row = lax.broadcasted_iota(jnp.int32, (TILE, TILE), 0)
    at_col = lax.broadcasted_iota(jnp.int32, (TILE, TILE), 1)
    eye = jnp.where(at_row == at_col, 1.0, 0.0).astype(BF)
    eye_half = eye[:CH, :CH]
    w_out_t[...] = dot_nt(eye_half, w_out[...]).astype(BF)
    grid_out_t[...] = dot_nt(eye_half, grid_out[...]).astype(BF)

    def prepare():
        block_out_t[...] = dot_nt(eye_half, block_out[...]).astype(BF)
        for ref, out in ((w_in, w_in_ct), (grid_in, grid_in_ct), (block_in, block_in_ct)):
            weight = ref[...].astype(F32)
            centered = (weight - jnp.mean(weight, axis=0, keepdims=True)).astype(BF)
            out[...] = dot_nt(eye, centered).astype(BF)
        grid_mix_t[...] = dot_nt(eye, grid_mix[...]).astype(BF)
        block_mix_t[...] = dot_nt(eye, block_mix[...]).astype(BF)

        def place(index):
            return (index & 15) * 16 + ((index >> 4) & 1) * 8 + (index >> 5)

        perm[...] = jnp.where(at_col == place(at_row), 1.0, 0.0).astype(BF)
        perm_t[...] = jnp.where(at_row == place(at_col), 1.0, 0.0).astype(BF)
        for ref in (a_grid_in, a_grid_out, a_block_in, a_block_mix, a_block_out, a_w_in, a_w_out):
            ref[...] = jnp.zeros_like(ref)

    feat_in.wait()
    cot_in.wait()
    prepare()
    lax.fori_loop(0, PRE_FIRST, lambda step, carry: (pre(step), carry)[1], 0)
    pl.semaphore_wait(barrier, DEVS - 1)
    pltpu.make_async_copy(sent.at[my_slot], there.at[me], there_sem).start()
    send_there(0, 1)
    lax.fori_loop(1, PRE_FIRST, lambda step, carry: (send_there(step, 0), carry)[1], 0)

    def pre_step(step, carry):
        pre(step)
        send_there(step, 0)
        return carry

    lax.fori_loop(PRE_FIRST, TILES, pre_step, 0)

    def block_step(tile, carry):
        n1 = n1_s[tile]
        cot_bf = tile_of(cot, tile)
        value, slope1 = gelu_both(dot(n1, w_in[:, CH:]))
        z_bf = value.astype(BF)
        upstream = dot(cot_bf, w_out_t[:, CH:]).astype(BF)
        normed, spread, gate, slope_gate, slope_mix, mix_spread, mix_input, d_gated, d_mixed = (
            branch_pre(z_bf, upstream, block_in, block_out_t)
        )
        mix_in = mix_input.astype(BF)
        d_mixed = d_mixed.astype(BF)
        mixed = dot(block_mix[...], mix_in)
        d_mix = dot(block_mix_t[...], d_mixed)
        a_block_mix[...] += dot_nt(d_mixed, mix_in)
        outcome, d_branch = branch_post(
            mixed, d_mix, z_bf, normed, spread, gate, slope_gate, slope_mix, mix_spread, mix_in,
            d_gated, upstream, block_in_ct, block_out, a_block_in, a_block_out,
        )
        joined_s[tile, :, CH:] = outcome
        a_w_out[CH:, :] += dot_tn(outcome, cot_bf)
        d_first = (d_branch * slope1).astype(BF)
        d_first_s[tile, :, CH:] = d_first
        a_w_in[:, CH:] += dot_tn(n1, d_first)
        return carry

    def block_pair(index, carry):
        block_step(index * 2, 0)
        block_step(index * 2 + 1, 0)
        return carry

    lax.fori_loop(0, TILES // 2, block_pair, 0)

    def pack(out, at, values):
        for left in range(0, values.shape[1], CH):
            count = values.shape[0] // 16
            piece = values[:, left : left + CH] * factor
            out[at : at + count] = piece.astype(BF).reshape(count, 16, CH)
            at += count
        return at

    def scatter(out, into, least, most, send, recv):
        def one(index, carry):
            chunk = least + lax.rem(index + me, most - least)
            to = lax.rem(chunk * SPREAD, DEVS)

            @pl.when(to != me)
            def _():
                pltpu.make_async_remote_copy(
                    src_ref=out.at[chunk],
                    dst_ref=into.at[me],
                    send_sem=send,
                    recv_sem=recv,
                    device_id=(to // COLS, lax.rem(to, COLS)),
                    device_id_type=MESH,
                ).start()

            return carry

        lax.fori_loop(0, most - least, one, 0)

    def gather(buffer, chunk, send, recv):
        def one(step, carry):
            pltpu.make_async_remote_copy(
                src_ref=buffer.at[chunk],
                dst_ref=buffer.at[chunk],
                send_sem=send,
                recv_sem=recv,
                device_id=peer_of(step),
                device_id_type=MESH,
            ).start()
            return carry

        lax.fori_loop(1, DEVS, one, 0)

    def wait_for(sem, buffer, count):
        pltpu.make_async_copy(
            buffer.at[pl.ds(0, count)], buffer.at[pl.ds(0, count)], sem
        ).wait()

    at = pack(early_out, 0, a_block_in[...])
    at = pack(early_out, at, a_block_mix[...])
    at = pack(early_out, at, a_block_out[...])
    at = pack(early_out, at, a_w_out[CH:, :])
    pack(early_out, at, a_w_in[:, CH:])
    scatter(early_out, early_in, 0, EARLY_A, send_sem.at[2], early_sem)

    wait_for(there_sem, there, DEVS)

    def gather_positions(row, carry):
        source = pl.ds(row * 16, 16)
        at = pl.ds(pl.multiple_of(row * 32, 32), 32)
        for part, out in ((0, x_mat), (16, d_mat)):
            values = there[source, part : part + 16, :].reshape(TILE, CH)
            values = dot(perm[...], values).astype(BF)
            for offset in range(8):
                out[at, offset * CH : (offset + 1) * CH] = values[offset * 32 : offset * 32 + 32]
        return carry

    lax.fori_loop(0, ROWS, gather_positions, 0, unroll=True)
    pack(early_out, EARLY_A, dot_nt(d_mat[...], x_mat[...]))
    scatter(early_out, early_in, EARLY_A, EARLY, send_sem.at[2], early_sem)
    x_mixed[...] = dot(grid_mix[...], x_mat[...]).astype(BF)
    d_mixed_back[...] = dot(grid_mix_t[...], d_mat[...]).astype(BF)

    def scatter_positions(row, carry):
        target = pl.ds(row * 16, 16)
        at = pl.ds(pl.multiple_of(row * 32, 32), 32)
        for part, src in ((0, x_mixed), (16, d_mixed_back)):
            values = jnp.concatenate(
                [src[at, offset * CH : (offset + 1) * CH] for offset in range(8)], axis=0
            )
            turned[target, part : part + 16, :] = (
                dot(perm_t[...], values).astype(BF).reshape(16, 16, CH)
            )
        return carry

    lax.fori_loop(0, ROWS, scatter_positions, 0, unroll=True)

    pltpu.make_async_copy(turned.at[me], back.at[my_slot], back_sem.at[pair]).start()

    def send_back(index, carry):
        tile = lax.rem(pair + index // 16, TILES)
        row = lax.rem(r + lax.rem(index, 16) // 2, ROWS)
        side = lax.rem(c + index, 2)
        col = tile * 2 + side
        pltpu.make_async_remote_copy(
            src_ref=turned.at[row * COLS + col],
            dst_ref=back.at[my_slot],
            send_sem=send_sem.at[1],
            recv_sem=back_sem.at[pair],
            device_id=(row, col),
            device_id_type=MESH,
        ).start()
        return carry

    lax.fori_loop(1, DEVS, send_back, 0)

    def reduce_chunk(out, into, every, chunk, send, recv, recv_all):
        into[me] = out[chunk]
        wait_for(recv, into, DEVS - 1)

        def add(index, total):
            return total + jnp.sum(into[pl.ds(index * 16, 16)].astype(F32), axis=0)

        total = lax.fori_loop(0, DEVS // 16, add, jnp.zeros((16, CH), F32))
        every[chunk] = total.astype(BF)
        gather(every, chunk, send, recv_all)

    def grid_step(step, carry):
        tile = lax.rem(pair + TILES - step, TILES)
        wait_for(back_sem.at[tile], back, 16)
        slots = pl.ds(tile * 16, 16)
        mixed = from_slots(back[slots, 0:16, :].reshape(TILE, CH).astype(F32))
        d_mix = from_slots(back[slots, 16:32, :].reshape(TILE, CH).astype(F32))
        cot_bf = tile_of(cot, tile)
        n1 = n1_s[tile]
        outcome, d_branch = branch_post(
            mixed, d_mix, z_s[tile], n2_s[tile], r2_s[tile], gate_s[tile],
            slope2_s[tile, :, :CH], slope2_s[tile, :, CH:], mix_r_s[tile], mix_s[tile],
            d_gated_s[tile], up_s[tile], grid_in_ct, grid_out, a_grid_in, a_grid_out,
        )
        joined_s[tile, :, :CH] = outcome
        a_w_out[:CH, :] += dot_tn(outcome, cot_bf)
        d_first = (d_branch * slope1_s[tile]).astype(BF)
        a_w_in[:, :CH] += dot_tn(n1, d_first)
        d_first_s[tile, :, :CH] = d_first
        return carry

    def output_step(tile, carry):
        x_bf = tile_of(feat, tile)
        cot_bf = tile_of(cot, tile)
        n1 = n1_s[tile]
        at = pl.ds(pl.multiple_of(tile * 16, 16), 16)
        out = (x_bf.astype(F32) + dot(joined_s[tile], w_out[...])).astype(BF)
        result_v[:, at, :] = out.reshape(16, 16, CH)
        g = dot(d_first_s[tile], w_in_ct[...])
        unit = n1.astype(F32)
        grad = cot_bf.astype(F32) + r1_s[tile] * (g - unit * row_mean(g * unit))
        feature_grad_v[:, at, :] = grad.astype(BF).reshape(16, 16, CH)
        return carry

    def output_pair(index, carry):
        output_step(index * 2, 0)
        output_step(index * 2 + 1, 0)
        return carry

    def grid_pair(index, carry):
        grid_step(index * 2, 0)
        grid_step(index * 2 + 1, 0)
        return carry

    lax.fori_loop(0, TILES // 2, grid_pair, 0)
    at = pack(late_out, 0, a_grid_in[...])
    at = pack(late_out, at, a_grid_out[...])
    at = pack(late_out, at, a_w_out[:CH, :])
    pack(late_out, at, a_w_in[:, :CH])
    scatter(late_out, late_in, 0, LATE, send_sem.at[4], late_sem)

    lax.fori_loop(0, TILES // 2, output_pair, 0)
    result_out = pltpu.make_async_copy(result_v, result, io_sem.at[2])
    feature_grad_out = pltpu.make_async_copy(feature_grad_v, feature_grad, io_sem.at[3])
    result_out.start()
    feature_grad_out.start()

    @pl.when(mine < EARLY)
    def _():
        reduce_chunk(
            early_out, early_in, early_all, mine, send_sem.at[3], early_sem, early_all_sem
        )

    @pl.when(mine < LATE)
    def _():
        reduce_chunk(
            late_out, late_in, late_all, mine, send_sem.at[5], late_sem, late_all_sem
        )

    @pl.when(mine < EARLY)
    def _():
        wait_for(early_all_sem, early_all, EARLY - 1)
        wait_for(send_sem.at[2], early_out, EARLY - 1)

    @pl.when(mine >= EARLY)
    def _():
        wait_for(early_all_sem, early_all, EARLY)
        wait_for(send_sem.at[2], early_out, EARLY)

    wait_for(send_sem.at[0], sent, DEVS - 1)
    wait_for(send_sem.at[1], turned, DEVS - 1)

    @pl.when(mine < EARLY)
    def _():
        wait_for(send_sem.at[3], early_in, DEVS - 1)

    @pl.when(mine >= LATE)
    def _():
        wait_for(late_all_sem, late_all, LATE)
        wait_for(send_sem.at[4], late_out, LATE)

    @pl.when(mine < LATE)
    def _():
        wait_for(late_all_sem, late_all, LATE - 1)
        wait_for(send_sem.at[4], late_out, LATE - 1)
        wait_for(send_sem.at[5], late_in, DEVS - 1)

    early_res[...] = early_all[...]
    late_res[...] = late_all[...]
    result_out.wait()
    feature_grad_out.wait()


def unpack(src, at, shape):
    halves = []
    for _ in range(0, shape[1], CH):
        count = shape[0] // 16
        halves.append(src[at : at + count].reshape(shape[0], CH).astype(F32))
        at += count
    return jnp.concatenate(halves, axis=1) if len(halves) > 1 else halves[0]


def finish(
    result_in, feature_grad_in, early_all, late_all,
    result, feature_grad, o_w_in, o_grid_in, o_grid_mix, o_grid_out, o_block_in, o_block_mix,
    o_block_out, o_w_out, sem,
):
    copies = [
        pltpu.make_async_copy(result_in, result, sem.at[0]),
        pltpu.make_async_copy(feature_grad_in, feature_grad, sem.at[1]),
    ]
    for copy in copies:
        copy.start()
    o_block_in[...] = unpack(early_all, 0, (128, 256))
    o_block_mix[...] = unpack(early_all, 16, (256, 256))
    o_block_out[...] = unpack(early_all, 48, (128, 128))
    o_w_out[CH:, :] = unpack(early_all, 56, (128, 128))
    o_w_in[:, CH:] = unpack(early_all, 64, (128, 128))
    o_grid_mix[...] = unpack(early_all, 72, (256, 256))
    o_grid_in[...] = unpack(late_all, 0, (128, 256))
    o_grid_out[...] = unpack(late_all, 16, (128, 128))
    o_w_out[:CH, :] = unpack(late_all, 24, (128, 128))
    o_w_in[:, :CH] = unpack(late_all, 32, (128, 128))
    for copy in copies:
        copy.wait()


def body(*args):
    def whole(dtype, *shape):
        return pltpu.VMEM(shape, dtype)

    pixels = (TILES, TILE, CH)
    both = (TILES, TILE, 2 * CH)
    scratch = [
        *[whole(BF, 16, 128, CH)] * 4,
        *[whole(BF, DEVS, 32, CH)] * 4,
        *[whole(BF, 256, 8 * CH)] * 4,
        whole(BF, *pixels),
        whole(F32, *pixels),
        whole(F32, *pixels),
        whole(BF, *pixels),
        whole(BF, *pixels),
        whole(F32, *pixels),
        whole(F32, *both),
        whole(F32, *pixels),
        whole(BF, *pixels),
        whole(F32, *pixels),
        whole(F32, *pixels),
        whole(BF, *pixels),
        whole(BF, *both),
        whole(BF, *both),
        *[whole(BF, TILE, TILE)] * 2,
        *[whole(BF, 2 * CH, CH)] * 3,
        *[whole(BF, 256, 256)] * 2,
        whole(BF, CH, 2 * CH),
        *[whole(BF, CH, CH)] * 2,
        whole(F32, CH, 2 * CH),
        whole(F32, CH, CH),
        whole(F32, CH, 2 * CH),
        whole(F32, 256, 256),
        whole(F32, CH, CH),
        whole(F32, CH, 2 * CH),
        whole(F32, 2 * CH, CH),
        whole(BF, EARLY, 16, CH),
        whole(BF, DEVS, 16, CH),
        whole(BF, EARLY, 16, CH),
        whole(BF, LATE, 16, CH),
        whole(BF, DEVS, 16, CH),
        whole(BF, LATE, 16, CH),
        pltpu.SemaphoreType.DMA((6,)),
        pltpu.SemaphoreType.DMA,
        pltpu.SemaphoreType.DMA((TILES,)),
        *[pltpu.SemaphoreType.DMA] * 4,
        pltpu.SemaphoreType.DMA((4,)),
    ]
    vmem = pl.BlockSpec(memory_space=pltpu.VMEM)
    shape = args[0].shape
    outs = [
        jax.ShapeDtypeStruct(shape, BF),
        jax.ShapeDtypeStruct(shape, BF),
        jax.ShapeDtypeStruct((128, 256), F32),
        jax.ShapeDtypeStruct((128, 256), F32),
        jax.ShapeDtypeStruct((256, 256), F32),
        jax.ShapeDtypeStruct((128, 128), F32),
        jax.ShapeDtypeStruct((128, 256), F32),
        jax.ShapeDtypeStruct((256, 256), F32),
        jax.ShapeDtypeStruct((128, 128), F32),
        jax.ShapeDtypeStruct((256, 128), F32),
    ]
    hbm = pl.BlockSpec(memory_space=pl.ANY)
    parts = pl.pallas_call(
        kernel,
        out_shape=[
            outs[0],
            outs[1],
            jax.ShapeDtypeStruct((EARLY, 16, CH), BF),
            jax.ShapeDtypeStruct((LATE, 16, CH), BF),
        ],
        in_specs=[hbm] * 2 + [vmem] * 8,
        out_specs=[hbm] * 2 + [vmem] * 2,
        scratch_shapes=scratch,
        compiler_params=pltpu.CompilerParams(
            collective_id=0, has_side_effects=True, vmem_limit_bytes=56 * 2**20
        ),
    )(*args)
    return tuple(
        pl.pallas_call(
            finish,
            out_shape=outs,
            in_specs=[vmem] * 4,
            out_specs=[hbm] * 2 + [vmem] * 8,
            scratch_shapes=[pltpu.SemaphoreType.DMA((2,))],
        )(*parts)
    )


def solution(mesh):
    split = P("row", "col", None)
    return jax.shard_map(
        body,
        mesh=mesh,
        in_specs=(split, split) + (P(),) * 8,
        out_specs=(split, split) + (P(),) * 8,
        check_vma=False,
    )
```

```python
import math

import jax
import jax.numpy as jnp
from jax import lax
from jax.experimental import pallas as pl
from jax.experimental.pallas import tpu as pltpu
from jax.sharding import PartitionSpec as P

MESH = pl.DeviceIdType.MESH
F32 = jnp.float32
BF = jnp.bfloat16

ROWS, COLS, CH = 8, 16, 128
DEVS = ROWS * COLS
TILES = 8
TILE = 256
EARLY_A = 72
EARLY = 104
LATE = 40
SPREAD = 3
UNSPREAD = 43
PRE_FIRST = 4

epsilon = 1e-06
tanh_scale = 0.7978845608028654
cubic = 0.044715


def dot(left, right):
    return jnp.dot(left, right, preferred_element_type=F32)


def dot_nt(left, right):
    return lax.dot_general(left, right, (((1,), (1,)), ((), ())), preferred_element_type=F32)


def dot_tn(left, right):
    return lax.dot_general(left, right, (((0,), (0,)), ((), ())), preferred_element_type=F32)


def gelu_both(hidden):
    square = hidden * hidden
    inner = jnp.tanh(hidden * (tanh_scale + (tanh_scale * cubic) * square))
    half = 0.5 + 0.5 * inner
    value = hidden * half
    slope = half + value * (1.0 - half) * (2.0 * tanh_scale + (6.0 * tanh_scale * cubic) * square)
    return value, slope


def to_slots(values):
    pieces = []
    for group in range(16):
        pieces.append(values[group * 8 : group * 8 + 8])
        pieces.append(values[128 + group * 8 : 128 + group * 8 + 8])
    return jnp.concatenate(pieces, axis=0)


def from_slots(values):
    pieces = [values[group * 16 : group * 16 + 8] for group in range(16)]
    pieces += [values[group * 16 + 8 : group * 16 + 16] for group in range(16)]
    return jnp.concatenate(pieces, axis=0)


def kernel(
    feat_hbm, cot_hbm, w_in, grid_in, grid_mix, grid_out, block_in, block_mix, block_out, w_out,
    result, feature_grad, early_res, late_res,
    feat, cot, result_v, feature_grad_v, sent, there, turned, back, x_mat, d_mat, x_mixed, d_mixed_back,
    n1_s, r1_s, slope1_s, z_s, n2_s, r2_s, slope2_s, gate_s, mix_s, mix_r_s, d_gated_s, up_s,
    joined_s, d_first_s,
    perm, perm_t, w_in_ct, grid_in_ct, block_in_ct, grid_mix_t, block_mix_t, w_out_t, grid_out_t,
    block_out_t,
    a_grid_in, a_grid_out, a_block_in, a_block_mix, a_block_out, a_w_in, a_w_out,
    early_out, early_in, early_all, late_out, late_in, late_all,
    send_sem, there_sem, back_sem, early_sem, early_all_sem, late_sem, late_all_sem, io_sem,
):
    factor = 1.0 / math.sqrt(DEVS * TILES * TILE)
    r = lax.axis_index("row")
    c = lax.axis_index("col")
    me = r * COLS + c
    mine = lax.rem(me * UNSPREAD, DEVS)
    pair = c // 2
    my_slot = pair * 16 + r * 2 + lax.rem(c, 2)

    def peer_of(step):
        row = lax.rem(r + lax.rem(step, ROWS), ROWS)
        col = lax.rem(c + step // ROWS, COLS)
        return row, col

    feat_in = pltpu.make_async_copy(feat_hbm, feat, io_sem.at[0])
    cot_in = pltpu.make_async_copy(cot_hbm, cot, io_sem.at[1])
    feat_in.start()
    cot_in.start()

    barrier = pltpu.get_barrier_semaphore()

    def greet(step, carry):
        pl.semaphore_signal(barrier, inc=1, device_id=peer_of(step), device_id_type=MESH)
        return carry

    lax.fori_loop(1, DEVS, greet, 0)

    def row_mean(values):
        return jnp.mean(values, axis=-1, keepdims=True)

    def normalize(values_bf):
        values = values_bf.astype(F32)
        center = values - row_mean(values)
        spread = lax.rsqrt(row_mean(center * center) + epsilon)
        return center * spread, spread

    def tile_of(ref, tile):
        at = pl.multiple_of(tile * 16, 16)
        return ref[:, pl.ds(at, 16), :].reshape(TILE, CH)

    def branch_pre(z_bf, upstream, in_weight, out_weight_t):
        unit, spread = normalize(z_bf)
        normed = unit.astype(BF)
        hidden = dot(normed, in_weight[...])
        gate, slope_gate = gelu_both(hidden[:, :CH])
        value, slope_mix = gelu_both(hidden[:, CH:])
        center = value - row_mean(value)
        mix_spread = lax.rsqrt(row_mean(center * center) + epsilon)
        mix_input = center * mix_spread
        d_gated = dot(upstream, out_weight_t[...])
        d_mixed = d_gated * gate
        return normed, spread, gate, slope_gate, slope_mix, mix_spread, mix_input, d_gated, d_mixed

    def branch_post(
        mixed, d_mix, z_bf, normed, spread, gate, slope_gate, slope_mix, mix_spread, mix_in,
        d_gated, upstream, in_centered_t, out_weight, acc_in, acc_out,
    ):
        mixed_one = mixed + 1.0
        gated = (gate * mixed_one).astype(BF)
        outcome = (z_bf.astype(F32) + dot(gated, out_weight[...])).astype(BF)
        acc_out[...] += dot_tn(gated, upstream)
        mix_unit = mix_in.astype(F32)
        d_value = mix_spread * (
            d_mix - row_mean(d_mix) - mix_unit * row_mean(d_mix * mix_unit)
        )
        d_hidden = jnp.concatenate(
            [(d_gated * mixed_one * slope_gate).astype(BF), (d_value * slope_mix).astype(BF)],
            axis=1,
        )
        acc_in[...] += dot_tn(normed, d_hidden)
        g = dot(d_hidden, in_centered_t[...])
        unit = normed.astype(F32)
        d_branch = upstream.astype(F32) + spread * (g - unit * row_mean(g * unit))
        return outcome, d_branch

    def pre(step):
        tile = lax.rem(pair + step, TILES)
        x_bf = tile_of(feat, tile)
        unit, spread = normalize(x_bf)
        n1 = unit.astype(BF)
        n1_s[tile] = n1
        r1_s[tile] = jnp.broadcast_to(spread, (TILE, CH))
        value, slope = gelu_both(dot(n1, w_in[:, :CH]))
        slope1_s[tile] = slope
        z_bf = value.astype(BF)
        z_s[tile] = z_bf
        upstream = dot(tile_of(cot, tile), w_out_t[:, :CH]).astype(BF)
        up_s[tile] = upstream
        normed, spread2, gate, slope_gate, slope_mix, mix_spread, mix_input, d_gated, d_mixed = (
            branch_pre(z_bf, upstream, grid_in, grid_out_t)
        )
        n2_s[tile] = normed
        r2_s[tile] = jnp.broadcast_to(spread2, (TILE, CH))
        gate_s[tile] = gate
        slope2_s[tile, :, :CH] = slope_gate
        slope2_s[tile, :, CH:] = slope_mix
        mix_r_s[tile] = jnp.broadcast_to(mix_spread, (TILE, CH))
        mix_s[tile] = mix_input.astype(BF)
        d_gated_s[tile] = d_gated
        slots = pl.ds(tile * 16, 16)
        sent[slots, 0:16, :] = to_slots(mix_input).astype(BF).reshape(16, 16, CH)
        sent[slots, 16:32, :] = to_slots(d_mixed).astype(BF).reshape(16, 16, CH)

    def send_there(step, first):
        tile = lax.rem(pair + step, TILES)

        def one(index, carry):
            row = lax.rem(r + index, ROWS)
            side = lax.rem(c + index // ROWS, 2)
            pltpu.make_async_remote_copy(
                src_ref=sent.at[tile * 16 + row * 2 + side],
                dst_ref=there.at[me],
                send_sem=send_sem.at[0],
                recv_sem=there_sem,
                device_id=(row, tile * 2 + side),
                device_id_type=MESH,
            ).start()
            return carry

        lax.fori_loop(first, 16, one, 0)

    at_row = lax.broadcasted_iota(jnp.int32, (TILE, TILE), 0)
    at_col = lax.broadcasted_iota(jnp.int32, (TILE, TILE), 1)
    eye = jnp.where(at_row == at_col, 1.0, 0.0).astype(BF)
    eye_half = eye[:CH, :CH]
    w_out_t[...] = dot_nt(eye_half, w_out[...]).astype(BF)
    grid_out_t[...] = dot_nt(eye_half, grid_out[...]).astype(BF)

    def prepare():
        block_out_t[...] = dot_nt(eye_half, block_out[...]).astype(BF)
        for ref, out in ((w_in, w_in_ct), (grid_in, grid_in_ct), (block_in, block_in_ct)):
            weight = ref[...].astype(F32)
            centered = (weight - jnp.mean(weight, axis=0, keepdims=True)).astype(BF)
            out[...] = dot_nt(eye, centered).astype(BF)
        grid_mix_t[...] = dot_nt(eye, grid_mix[...]).astype(BF)
        block_mix_t[...] = dot_nt(eye, block_mix[...]).astype(BF)

        def place(index):
            return (index & 15) * 16 + ((index >> 4) & 1) * 8 + (index >> 5)

        perm[...] = jnp.where(at_col == place(at_row), 1.0, 0.0).astype(BF)
        perm_t[...] = jnp.where(at_row == place(at_col), 1.0, 0.0).astype(BF)
        for ref in (a_grid_in, a_grid_out, a_block_in, a_block_mix, a_block_out, a_w_in, a_w_out):
            ref[...] = jnp.zeros_like(ref)

    feat_in.wait()
    cot_in.wait()
    prepare()
    lax.fori_loop(0, PRE_FIRST, lambda step, carry: (pre(step), carry)[1], 0)
    pl.semaphore_wait(barrier, DEVS - 1)
    pltpu.make_async_copy(sent.at[my_slot], there.at[me], there_sem).start()
    send_there(0, 1)
    lax.fori_loop(1, PRE_FIRST, lambda step, carry: (send_there(step, 0), carry)[1], 0)

    def pre_step(step, carry):
        pre(step)
        send_there(step, 0)
        return carry

    lax.fori_loop(PRE_FIRST, TILES, pre_step, 0)

    def block_step(tile, carry):
        n1 = n1_s[tile]
        cot_bf = tile_of(cot, tile)
        value, slope1 = gelu_both(dot(n1, w_in[:, CH:]))
        z_bf = value.astype(BF)
        upstream = dot(cot_bf, w_out_t[:, CH:]).astype(BF)
        normed, spread, gate, slope_gate, slope_mix, mix_spread, mix_input, d_gated, d_mixed = (
            branch_pre(z_bf, upstream, block_in, block_out_t)
        )
        mix_in = mix_input.astype(BF)
        d_mixed = d_mixed.astype(BF)
        mixed = dot(block_mix[...], mix_in)
        d_mix = dot(block_mix_t[...], d_mixed)
        a_block_mix[...] += dot_nt(d_mixed, mix_in)
        outcome, d_branch = branch_post(
            mixed, d_mix, z_bf, normed, spread, gate, slope_gate, slope_mix, mix_spread, mix_in,
            d_gated, upstream, block_in_ct, block_out, a_block_in, a_block_out,
        )
        joined_s[tile, :, CH:] = outcome
        a_w_out[CH:, :] += dot_tn(outcome, cot_bf)
        d_first = (d_branch * slope1).astype(BF)
        d_first_s[tile, :, CH:] = d_first
        a_w_in[:, CH:] += dot_tn(n1, d_first)
        return carry

    def block_pair(index, carry):
        block_step(index * 2, 0)
        block_step(index * 2 + 1, 0)
        return carry

    lax.fori_loop(0, TILES // 2, block_pair, 0)

    def pack(out, at, values):
        for left in range(0, values.shape[1], CH):
            count = values.shape[0] // 16
            piece = values[:, left : left + CH] * factor
            out[at : at + count] = piece.astype(BF).reshape(count, 16, CH)
            at += count
        return at

    def scatter(out, into, least, most, send, recv):
        def one(index, carry):
            chunk = least + lax.rem(index + me, most - least)
            to = lax.rem(chunk * SPREAD, DEVS)

            @pl.when(to != me)
            def _():
                pltpu.make_async_remote_copy(
                    src_ref=out.at[chunk],
                    dst_ref=into.at[me],
                    send_sem=send,
                    recv_sem=recv,
                    device_id=(to // COLS, lax.rem(to, COLS)),
                    device_id_type=MESH,
                ).start()

            return carry

        lax.fori_loop(0, most - least, one, 0)

    def gather(buffer, chunk, send, recv):
        def one(step, carry):
            pltpu.make_async_remote_copy(
                src_ref=buffer.at[chunk],
                dst_ref=buffer.at[chunk],
                send_sem=send,
                recv_sem=recv,
                device_id=peer_of(step),
                device_id_type=MESH,
            ).start()
            return carry

        lax.fori_loop(1, DEVS, one, 0)

    def wait_for(sem, buffer, count):
        pltpu.make_async_copy(
            buffer.at[pl.ds(0, count)], buffer.at[pl.ds(0, count)], sem
        ).wait()

    at = pack(early_out, 0, a_block_in[...])
    at = pack(early_out, at, a_block_mix[...])
    at = pack(early_out, at, a_block_out[...])
    at = pack(early_out, at, a_w_out[CH:, :])
    pack(early_out, at, a_w_in[:, CH:])
    scatter(early_out, early_in, 0, EARLY_A, send_sem.at[2], early_sem)

    wait_for(there_sem, there, DEVS)

    def gather_positions(row, carry):
        source = pl.ds(row * 16, 16)
        at = pl.ds(pl.multiple_of(row * 32, 32), 32)
        for part, out in ((0, x_mat), (16, d_mat)):
            values = there[source, part : part + 16, :].reshape(TILE, CH)
            values = dot(perm[...], values).astype(BF)
            for offset in range(8):
                out[at, offset * CH : (offset + 1) * CH] = values[offset * 32 : offset * 32 + 32]
        return carry

    lax.fori_loop(0, ROWS, gather_positions, 0, unroll=True)
    pack(early_out, EARLY_A, dot_nt(d_mat[...], x_mat[...]))
    scatter(early_out, early_in, EARLY_A, EARLY, send_sem.at[2], early_sem)
    x_mixed[...] = dot(grid_mix[...], x_mat[...]).astype(BF)
    d_mixed_back[...] = dot(grid_mix_t[...], d_mat[...]).astype(BF)

    def scatter_positions(row, carry):
        target = pl.ds(row * 16, 16)
        at = pl.ds(pl.multiple_of(row * 32, 32), 32)
        for part, src in ((0, x_mixed), (16, d_mixed_back)):
            values = jnp.concatenate(
                [src[at, offset * CH : (offset + 1) * CH] for offset in range(8)], axis=0
            )
            turned[target, part : part + 16, :] = (
                dot(perm_t[...], values).astype(BF).reshape(16, 16, CH)
            )
        return carry

    lax.fori_loop(0, ROWS, scatter_positions, 0, unroll=True)

    pltpu.make_async_copy(turned.at[me], back.at[my_slot], back_sem.at[pair]).start()

    def send_back(index, carry):
        tile = lax.rem(pair + index // 16, TILES)
        row = lax.rem(r + index, ROWS)
        side = lax.rem(c + index // ROWS, 2)
        col = tile * 2 + side
        pltpu.make_async_remote_copy(
            src_ref=turned.at[row * COLS + col],
            dst_ref=back.at[my_slot],
            send_sem=send_sem.at[1],
            recv_sem=back_sem.at[pair],
            device_id=(row, col),
            device_id_type=MESH,
        ).start()
        return carry

    lax.fori_loop(1, DEVS, send_back, 0)

    def reduce_chunk(out, into, every, chunk, send, recv, recv_all):
        into[me] = out[chunk]
        wait_for(recv, into, DEVS - 1)

        def add(index, total):
            return total + jnp.sum(into[pl.ds(index * 16, 16)].astype(F32), axis=0)

        total = lax.fori_loop(0, DEVS // 16, add, jnp.zeros((16, CH), F32), unroll=True)
        every[chunk] = total.astype(BF)
        gather(every, chunk, send, recv_all)

    def grid_step(step, carry):
        tile = lax.rem(pair + TILES - step, TILES)
        wait_for(back_sem.at[tile], back, 16)
        slots = pl.ds(tile * 16, 16)
        mixed = from_slots(back[slots, 0:16, :].reshape(TILE, CH).astype(F32))
        d_mix = from_slots(back[slots, 16:32, :].reshape(TILE, CH).astype(F32))
        cot_bf = tile_of(cot, tile)
        n1 = n1_s[tile]
        outcome, d_branch = branch_post(
            mixed, d_mix, z_s[tile], n2_s[tile], r2_s[tile], gate_s[tile],
            slope2_s[tile, :, :CH], slope2_s[tile, :, CH:], mix_r_s[tile], mix_s[tile],
            d_gated_s[tile], up_s[tile], grid_in_ct, grid_out, a_grid_in, a_grid_out,
        )
        joined_s[tile, :, :CH] = outcome
        a_w_out[:CH, :] += dot_tn(outcome, cot_bf)
        d_first = (d_branch * slope1_s[tile]).astype(BF)
        a_w_in[:, :CH] += dot_tn(n1, d_first)
        d_first_s[tile, :, :CH] = d_first
        return carry

    def output_step(tile, carry):
        x_bf = tile_of(feat, tile)
        cot_bf = tile_of(cot, tile)
        n1 = n1_s[tile]
        at = pl.ds(pl.multiple_of(tile * 16, 16), 16)
        out = (x_bf.astype(F32) + dot(joined_s[tile], w_out[...])).astype(BF)
        result_v[:, at, :] = out.reshape(16, 16, CH)
        g = dot(d_first_s[tile], w_in_ct[...])
        unit = n1.astype(F32)
        grad = cot_bf.astype(F32) + r1_s[tile] * (g - unit * row_mean(g * unit))
        feature_grad_v[:, at, :] = grad.astype(BF).reshape(16, 16, CH)
        return carry

    def output_pair(index, carry):
        output_step(index * 2, 0)
        output_step(index * 2 + 1, 0)
        return carry

    def grid_pair(index, carry):
        grid_step(index * 2, 0)
        grid_step(index * 2 + 1, 0)
        return carry

    lax.fori_loop(0, TILES // 2, grid_pair, 0)
    at = pack(late_out, 0, a_grid_in[...])
    at = pack(late_out, at, a_grid_out[...])
    at = pack(late_out, at, a_w_out[:CH, :])
    pack(late_out, at, a_w_in[:, :CH])
    scatter(late_out, late_in, 0, LATE, send_sem.at[4], late_sem)

    lax.fori_loop(0, TILES // 2, output_pair, 0)
    result_out = pltpu.make_async_copy(result_v, result, io_sem.at[2])
    feature_grad_out = pltpu.make_async_copy(feature_grad_v, feature_grad, io_sem.at[3])
    result_out.start()
    feature_grad_out.start()

    @pl.when(mine < EARLY)
    def _():
        reduce_chunk(
            early_out, early_in, early_all, mine, send_sem.at[3], early_sem, early_all_sem
        )

    @pl.when(mine < LATE)
    def _():
        reduce_chunk(
            late_out, late_in, late_all, mine, send_sem.at[5], late_sem, late_all_sem
        )

    @pl.when(mine < EARLY)
    def _():
        wait_for(early_all_sem, early_all, EARLY - 1)
        wait_for(send_sem.at[2], early_out, EARLY - 1)

    @pl.when(mine >= EARLY)
    def _():
        wait_for(early_all_sem, early_all, EARLY)
        wait_for(send_sem.at[2], early_out, EARLY)

    wait_for(send_sem.at[0], sent, DEVS - 1)
    wait_for(send_sem.at[1], turned, DEVS - 1)

    @pl.when(mine < EARLY)
    def _():
        wait_for(send_sem.at[3], early_in, DEVS - 1)

    @pl.when(mine >= LATE)
    def _():
        wait_for(late_all_sem, late_all, LATE)
        wait_for(send_sem.at[4], late_out, LATE)

    @pl.when(mine < LATE)
    def _():
        wait_for(late_all_sem, late_all, LATE - 1)
        wait_for(send_sem.at[4], late_out, LATE - 1)
        wait_for(send_sem.at[5], late_in, DEVS - 1)

    early_res[...] = early_all[...]
    late_res[...] = late_all[...]
    result_out.wait()
    feature_grad_out.wait()


def unpack(src, at, shape):
    halves = []
    for _ in range(0, shape[1], CH):
        count = shape[0] // 16
        halves.append(src[at : at + count].reshape(shape[0], CH).astype(F32))
        at += count
    return jnp.concatenate(halves, axis=1) if len(halves) > 1 else halves[0]


def finish(
    result_in, feature_grad_in, early_in, late_in,
    result, feature_grad, o_w_in, o_grid_in, o_grid_mix, o_grid_out, o_block_in, o_block_mix,
    o_block_out, o_w_out, result_v, feature_grad_v, early_all, late_all, sem,
):
    arrivals = [
        pltpu.make_async_copy(result_in, result_v, sem.at[0]),
        pltpu.make_async_copy(feature_grad_in, feature_grad_v, sem.at[1]),
        pltpu.make_async_copy(early_in, early_all, sem.at[2]),
        pltpu.make_async_copy(late_in, late_all, sem.at[3]),
    ]
    copies = [
        pltpu.make_async_copy(result_v, result, sem.at[4]),
        pltpu.make_async_copy(feature_grad_v, feature_grad, sem.at[5]),
    ]
    for arrival in arrivals:
        arrival.start()
    for arrival, copy in zip(arrivals, copies):
        arrival.wait()
        copy.start()
    arrivals[2].wait()
    arrivals[3].wait()
    o_block_in[...] = unpack(early_all, 0, (128, 256))
    o_block_mix[...] = unpack(early_all, 16, (256, 256))
    o_block_out[...] = unpack(early_all, 48, (128, 128))
    o_w_out[CH:, :] = unpack(early_all, 56, (128, 128))
    o_w_in[:, CH:] = unpack(early_all, 64, (128, 128))
    o_grid_mix[...] = unpack(early_all, 72, (256, 256))
    o_grid_in[...] = unpack(late_all, 0, (128, 256))
    o_grid_out[...] = unpack(late_all, 16, (128, 128))
    o_w_out[:CH, :] = unpack(late_all, 24, (128, 128))
    o_w_in[:, :CH] = unpack(late_all, 32, (128, 128))
    for copy in copies:
        copy.wait()


def body(*args):
    def whole(dtype, *shape):
        return pltpu.VMEM(shape, dtype)

    pixels = (TILES, TILE, CH)
    both = (TILES, TILE, 2 * CH)
    scratch = [
        *[whole(BF, 16, 128, CH)] * 4,
        *[whole(BF, DEVS, 32, CH)] * 4,
        *[whole(BF, 256, 8 * CH)] * 4,
        whole(BF, *pixels),
        whole(F32, *pixels),
        whole(F32, *pixels),
        whole(BF, *pixels),
        whole(BF, *pixels),
        whole(F32, *pixels),
        whole(F32, *both),
        whole(F32, *pixels),
        whole(BF, *pixels),
        whole(F32, *pixels),
        whole(F32, *pixels),
        whole(BF, *pixels),
        whole(BF, *both),
        whole(BF, *both),
        *[whole(BF, TILE, TILE)] * 2,
        *[whole(BF, 2 * CH, CH)] * 3,
        *[whole(BF, 256, 256)] * 2,
        whole(BF, CH, 2 * CH),
        *[whole(BF, CH, CH)] * 2,
        whole(F32, CH, 2 * CH),
        whole(F32, CH, CH),
        whole(F32, CH, 2 * CH),
        whole(F32, 256, 256),
        whole(F32, CH, CH),
        whole(F32, CH, 2 * CH),
        whole(F32, 2 * CH, CH),
        whole(BF, EARLY, 16, CH),
        whole(BF, DEVS, 16, CH),
        whole(BF, EARLY, 16, CH),
        whole(BF, LATE, 16, CH),
        whole(BF, DEVS, 16, CH),
        whole(BF, LATE, 16, CH),
        pltpu.SemaphoreType.DMA((6,)),
        pltpu.SemaphoreType.DMA,
        pltpu.SemaphoreType.DMA((TILES,)),
        *[pltpu.SemaphoreType.DMA] * 4,
        pltpu.SemaphoreType.DMA((4,)),
    ]
    vmem = pl.BlockSpec(memory_space=pltpu.VMEM)
    shape = args[0].shape
    outs = [
        jax.ShapeDtypeStruct(shape, BF),
        jax.ShapeDtypeStruct(shape, BF),
        jax.ShapeDtypeStruct((128, 256), F32),
        jax.ShapeDtypeStruct((128, 256), F32),
        jax.ShapeDtypeStruct((256, 256), F32),
        jax.ShapeDtypeStruct((128, 128), F32),
        jax.ShapeDtypeStruct((128, 256), F32),
        jax.ShapeDtypeStruct((256, 256), F32),
        jax.ShapeDtypeStruct((128, 128), F32),
        jax.ShapeDtypeStruct((256, 128), F32),
    ]
    hbm = pl.BlockSpec(memory_space=pl.ANY)
    parts = pl.pallas_call(
        kernel,
        out_shape=[
            outs[0],
            outs[1],
            jax.ShapeDtypeStruct((EARLY, 16, CH), BF),
            jax.ShapeDtypeStruct((LATE, 16, CH), BF),
        ],
        in_specs=[hbm] * 2 + [vmem] * 8,
        out_specs=[hbm] * 2 + [vmem] * 2,
        scratch_shapes=scratch,
        compiler_params=pltpu.CompilerParams(
            collective_id=0, has_side_effects=True, vmem_limit_bytes=56 * 2**20
        ),
    )(*args)
    return tuple(
        pl.pallas_call(
            finish,
            out_shape=outs,
            in_specs=[hbm] * 4,
            out_specs=[hbm] * 2 + [vmem] * 8,
            scratch_shapes=[
                pltpu.VMEM(shape, BF),
                pltpu.VMEM(shape, BF),
                pltpu.VMEM(parts[2].shape, BF),
                pltpu.VMEM(parts[3].shape, BF),
                pltpu.SemaphoreType.DMA((6,)),
            ],
        )(*parts)
    )


def solution(mesh):
    split = P("row", "col", None)
    return jax.shard_map(
        body,
        mesh=mesh,
        in_specs=(split, split) + (P(),) * 8,
        out_specs=(split, split) + (P(),) * 8,
        check_vma=False,
    )
```

```python
import math

import jax
import jax.numpy as jnp
from jax import lax
from jax.experimental import pallas as pl
from jax.experimental.pallas import tpu as pltpu
from jax.sharding import PartitionSpec as P

MESH = pl.DeviceIdType.MESH
F32 = jnp.float32
BF = jnp.bfloat16

ROWS, COLS, CH = 8, 16, 128
DEVS = ROWS * COLS
TILES = 8
TILE = 256
EARLY_A = 72
EARLY = 104
LATE = 40
SPREAD = 3
UNSPREAD = 43
PRE_FIRST = 4

epsilon = 1e-06
tanh_scale = 0.7978845608028654
cubic = 0.044715


def dot(left, right):
    return jnp.dot(left, right, preferred_element_type=F32)


def dot_nt(left, right):
    return lax.dot_general(left, right, (((1,), (1,)), ((), ())), preferred_element_type=F32)


def dot_tn(left, right):
    return lax.dot_general(left, right, (((0,), (0,)), ((), ())), preferred_element_type=F32)


def gelu_both(hidden):
    square = hidden * hidden
    inner = jnp.tanh(hidden * (tanh_scale + (tanh_scale * cubic) * square))
    half = 0.5 + 0.5 * inner
    value = hidden * half
    slope = half + value * (1.0 - half) * (2.0 * tanh_scale + (6.0 * tanh_scale * cubic) * square)
    return value, slope


def to_slots(values):
    pieces = []
    for group in range(16):
        pieces.append(values[group * 8 : group * 8 + 8])
        pieces.append(values[128 + group * 8 : 128 + group * 8 + 8])
    return jnp.concatenate(pieces, axis=0)


def from_slots(values):
    pieces = [values[group * 16 : group * 16 + 8] for group in range(16)]
    pieces += [values[group * 16 + 8 : group * 16 + 16] for group in range(16)]
    return jnp.concatenate(pieces, axis=0)


def kernel(
    feat_hbm, cot_hbm, w_in, grid_in, grid_mix, grid_out, block_in, block_mix, block_out, w_out,
    result, feature_grad, early_res, late_res,
    feat, cot, result_v, feature_grad_v, sent, there, turned, back, x_mat, d_mat, x_mixed, d_mixed_back,
    n1_s, r1_s, slope1_s, z_s, n2_s, r2_s, slope2_s, gate_s, mix_s, mix_r_s, d_gated_s, up_s,
    joined_s, d_first_s,
    perm, perm_t, w_in_ct, grid_in_ct, block_in_ct, grid_mix_t, block_mix_t, w_out_t, grid_out_t,
    block_out_t,
    a_grid_in, a_grid_out, a_block_in, a_block_mix, a_block_out, a_w_in, a_w_out,
    early_out, early_in, early_all, late_out, late_in, late_all,
    send_sem, there_sem, back_sem, early_sem, early_all_sem, late_sem, late_all_sem, io_sem,
):
    factor = 1.0 / math.sqrt(DEVS * TILES * TILE)
    r = lax.axis_index("row")
    c = lax.axis_index("col")
    me = r * COLS + c
    mine = lax.rem(me * UNSPREAD, DEVS)
    pair = c // 2
    my_slot = pair * 16 + r * 2 + lax.rem(c, 2)

    def peer_of(step):
        row = lax.rem(r + lax.rem(step, ROWS), ROWS)
        col = lax.rem(c + step // ROWS, COLS)
        return row, col

    feat_in = pltpu.make_async_copy(feat_hbm, feat, io_sem.at[0])
    cot_in = pltpu.make_async_copy(cot_hbm, cot, io_sem.at[1])
    feat_in.start()
    cot_in.start()

    barrier = pltpu.get_barrier_semaphore()

    def greet(step, carry):
        pl.semaphore_signal(barrier, inc=1, device_id=peer_of(step), device_id_type=MESH)
        return carry

    lax.fori_loop(1, DEVS, greet, 0, unroll=8)

    def row_mean(values):
        return jnp.mean(values, axis=-1, keepdims=True)

    def normalize(values_bf):
        values = values_bf.astype(F32)
        center = values - row_mean(values)
        spread = lax.rsqrt(row_mean(center * center) + epsilon)
        return center * spread, spread

    def tile_of(ref, tile):
        at = pl.multiple_of(tile * 16, 16)
        return ref[:, pl.ds(at, 16), :].reshape(TILE, CH)

    def branch_pre(z_bf, upstream, in_weight, out_weight_t):
        unit, spread = normalize(z_bf)
        normed = unit.astype(BF)
        hidden = dot(normed, in_weight[...])
        gate, slope_gate = gelu_both(hidden[:, :CH])
        value, slope_mix = gelu_both(hidden[:, CH:])
        center = value - row_mean(value)
        mix_spread = lax.rsqrt(row_mean(center * center) + epsilon)
        mix_input = center * mix_spread
        d_gated = dot(upstream, out_weight_t[...])
        d_mixed = d_gated * gate
        return normed, spread, gate, slope_gate, slope_mix, mix_spread, mix_input, d_gated, d_mixed

    def branch_post(
        mixed, d_mix, z_bf, normed, spread, gate, slope_gate, slope_mix, mix_spread, mix_in,
        d_gated, upstream, in_centered_t, out_weight, acc_in, acc_out,
    ):
        mixed_one = mixed + 1.0
        gated = (gate * mixed_one).astype(BF)
        outcome = (z_bf.astype(F32) + dot(gated, out_weight[...])).astype(BF)
        acc_out[...] += dot_tn(gated, upstream)
        mix_unit = mix_in.astype(F32)
        d_value = mix_spread * (
            d_mix - row_mean(d_mix) - mix_unit * row_mean(d_mix * mix_unit)
        )
        d_hidden = jnp.concatenate(
            [(d_gated * mixed_one * slope_gate).astype(BF), (d_value * slope_mix).astype(BF)],
            axis=1,
        )
        acc_in[...] += dot_tn(normed, d_hidden)
        g = dot(d_hidden, in_centered_t[...])
        unit = normed.astype(F32)
        d_branch = upstream.astype(F32) + spread * (g - unit * row_mean(g * unit))
        return outcome, d_branch

    def pre(step):
        tile = lax.rem(pair + step, TILES)
        x_bf = tile_of(feat, tile)
        unit, spread = normalize(x_bf)
        n1 = unit.astype(BF)
        n1_s[tile] = n1
        r1_s[tile] = jnp.broadcast_to(spread, (TILE, CH))
        value, slope = gelu_both(dot(n1, w_in[:, :CH]))
        slope1_s[tile] = slope
        z_bf = value.astype(BF)
        z_s[tile] = z_bf
        upstream = dot(tile_of(cot, tile), w_out_t[:, :CH]).astype(BF)
        up_s[tile] = upstream
        normed, spread2, gate, slope_gate, slope_mix, mix_spread, mix_input, d_gated, d_mixed = (
            branch_pre(z_bf, upstream, grid_in, grid_out_t)
        )
        n2_s[tile] = normed
        r2_s[tile] = jnp.broadcast_to(spread2, (TILE, CH))
        gate_s[tile] = gate
        slope2_s[tile, :, :CH] = slope_gate
        slope2_s[tile, :, CH:] = slope_mix
        mix_r_s[tile] = jnp.broadcast_to(mix_spread, (TILE, CH))
        mix_s[tile] = mix_input.astype(BF)
        d_gated_s[tile] = d_gated
        slots = pl.ds(tile * 16, 16)
        sent[slots, 0:16, :] = to_slots(mix_input).astype(BF).reshape(16, 16, CH)
        sent[slots, 16:32, :] = to_slots(d_mixed).astype(BF).reshape(16, 16, CH)

    def send_there(step, first):
        tile = lax.rem(pair + step, TILES)

        def one(index, carry):
            row = lax.rem(r + index, ROWS)
            side = lax.rem(c + index // ROWS, 2)
            pltpu.make_async_remote_copy(
                src_ref=sent.at[tile * 16 + row * 2 + side],
                dst_ref=there.at[me],
                send_sem=send_sem.at[0],
                recv_sem=there_sem,
                device_id=(row, tile * 2 + side),
                device_id_type=MESH,
            ).start()
            return carry

        lax.fori_loop(first, 16, one, 0)

    at_row = lax.broadcasted_iota(jnp.int32, (TILE, TILE), 0)
    at_col = lax.broadcasted_iota(jnp.int32, (TILE, TILE), 1)
    eye = jnp.where(at_row == at_col, 1.0, 0.0).astype(BF)
    eye_half = eye[:CH, :CH]
    w_out_t[...] = dot_nt(eye_half, w_out[...]).astype(BF)
    grid_out_t[...] = dot_nt(eye_half, grid_out[...]).astype(BF)

    def prepare():
        block_out_t[...] = dot_nt(eye_half, block_out[...]).astype(BF)
        for ref, out in ((w_in, w_in_ct), (grid_in, grid_in_ct), (block_in, block_in_ct)):
            weight = ref[...].astype(F32)
            centered = (weight - jnp.mean(weight, axis=0, keepdims=True)).astype(BF)
            out[...] = dot_nt(eye, centered).astype(BF)
        grid_mix_t[...] = dot_nt(eye, grid_mix[...]).astype(BF)
        block_mix_t[...] = dot_nt(eye, block_mix[...]).astype(BF)

        def place(index):
            return (index & 15) * 16 + ((index >> 4) & 1) * 8 + (index >> 5)

        perm[...] = jnp.where(at_col == place(at_row), 1.0, 0.0).astype(BF)
        perm_t[...] = jnp.where(at_row == place(at_col), 1.0, 0.0).astype(BF)
        for ref in (a_grid_in, a_grid_out, a_block_in, a_block_mix, a_block_out, a_w_in, a_w_out):
            ref[...] = jnp.zeros_like(ref)

    feat_in.wait()
    cot_in.wait()
    prepare()
    lax.fori_loop(0, PRE_FIRST, lambda step, carry: (pre(step), carry)[1], 0)
    pl.semaphore_wait(barrier, DEVS - 1)
    pltpu.make_async_copy(sent.at[my_slot], there.at[me], there_sem).start()
    send_there(0, 1)
    lax.fori_loop(1, PRE_FIRST, lambda step, carry: (send_there(step, 0), carry)[1], 0)

    def pre_step(step, carry):
        pre(step)
        send_there(step, 0)
        return carry

    lax.fori_loop(PRE_FIRST, TILES, pre_step, 0)

    def block_step(tile, carry):
        n1 = n1_s[tile]
        cot_bf = tile_of(cot, tile)
        value, slope1 = gelu_both(dot(n1, w_in[:, CH:]))
        z_bf = value.astype(BF)
        upstream = dot(cot_bf, w_out_t[:, CH:]).astype(BF)
        normed, spread, gate, slope_gate, slope_mix, mix_spread, mix_input, d_gated, d_mixed = (
            branch_pre(z_bf, upstream, block_in, block_out_t)
        )
        mix_in = mix_input.astype(BF)
        d_mixed = d_mixed.astype(BF)
        mixed = dot(block_mix[...], mix_in)
        d_mix = dot(block_mix_t[...], d_mixed)
        a_block_mix[...] += dot_nt(d_mixed, mix_in)
        outcome, d_branch = branch_post(
            mixed, d_mix, z_bf, normed, spread, gate, slope_gate, slope_mix, mix_spread, mix_in,
            d_gated, upstream, block_in_ct, block_out, a_block_in, a_block_out,
        )
        joined_s[tile, :, CH:] = outcome
        a_w_out[CH:, :] += dot_tn(outcome, cot_bf)
        d_first = (d_branch * slope1).astype(BF)
        d_first_s[tile, :, CH:] = d_first
        a_w_in[:, CH:] += dot_tn(n1, d_first)
        return carry

    def block_pair(index, carry):
        block_step(index * 2, 0)
        block_step(index * 2 + 1, 0)
        return carry

    lax.fori_loop(0, TILES // 2, block_pair, 0)

    def pack(out, at, values):
        for left in range(0, values.shape[1], CH):
            count = values.shape[0] // 16
            piece = values[:, left : left + CH] * factor
            out[at : at + count] = piece.astype(BF).reshape(count, 16, CH)
            at += count
        return at

    def scatter(out, into, least, most, send, recv):
        def one(index, carry):
            chunk = least + lax.rem(index + me, most - least)
            to = lax.rem(chunk * SPREAD, DEVS)

            @pl.when(to != me)
            def _():
                pltpu.make_async_remote_copy(
                    src_ref=out.at[chunk],
                    dst_ref=into.at[me],
                    send_sem=send,
                    recv_sem=recv,
                    device_id=(to // COLS, lax.rem(to, COLS)),
                    device_id_type=MESH,
                ).start()

            return carry

        lax.fori_loop(0, most - least, one, 0)

    def gather(buffer, chunk, send, recv):
        def one(step, carry):
            pltpu.make_async_remote_copy(
                src_ref=buffer.at[chunk],
                dst_ref=buffer.at[chunk],
                send_sem=send,
                recv_sem=recv,
                device_id=peer_of(step),
                device_id_type=MESH,
            ).start()
            return carry

        lax.fori_loop(1, DEVS, one, 0, unroll=8)

    def wait_for(sem, buffer, count):
        pltpu.make_async_copy(
            buffer.at[pl.ds(0, count)], buffer.at[pl.ds(0, count)], sem
        ).wait()

    at = pack(early_out, 0, a_block_in[...])
    at = pack(early_out, at, a_block_mix[...])
    at = pack(early_out, at, a_block_out[...])
    at = pack(early_out, at, a_w_out[CH:, :])
    pack(early_out, at, a_w_in[:, CH:])
    scatter(early_out, early_in, 0, EARLY_A, send_sem.at[2], early_sem)

    wait_for(there_sem, there, DEVS)

    def gather_positions(row, carry):
        source = pl.ds(row * 16, 16)
        at = pl.ds(pl.multiple_of(row * 32, 32), 32)
        for part, out in ((0, x_mat), (16, d_mat)):
            values = there[source, part : part + 16, :].reshape(TILE, CH)
            values = dot(perm[...], values).astype(BF)
            for offset in range(8):
                out[at, offset * CH : (offset + 1) * CH] = values[offset * 32 : offset * 32 + 32]
        return carry

    lax.fori_loop(0, ROWS, gather_positions, 0, unroll=True)
    pack(early_out, EARLY_A, dot_nt(d_mat[...], x_mat[...]))
    scatter(early_out, early_in, EARLY_A, EARLY, send_sem.at[2], early_sem)
    x_mixed[...] = dot(grid_mix[...], x_mat[...]).astype(BF)
    d_mixed_back[...] = dot(grid_mix_t[...], d_mat[...]).astype(BF)

    def scatter_positions(row, carry):
        target = pl.ds(row * 16, 16)
        at = pl.ds(pl.multiple_of(row * 32, 32), 32)
        for part, src in ((0, x_mixed), (16, d_mixed_back)):
            values = jnp.concatenate(
                [src[at, offset * CH : (offset + 1) * CH] for offset in range(8)], axis=0
            )
            turned[target, part : part + 16, :] = (
                dot(perm_t[...], values).astype(BF).reshape(16, 16, CH)
            )
        return carry

    lax.fori_loop(0, ROWS, scatter_positions, 0, unroll=True)

    pltpu.make_async_copy(turned.at[me], back.at[my_slot], back_sem.at[pair]).start()

    def send_back(index, carry):
        tile = lax.rem(pair + index // 16, TILES)
        row = lax.rem(r + index, ROWS)
        side = lax.rem(c + index // ROWS, 2)
        col = tile * 2 + side
        pltpu.make_async_remote_copy(
            src_ref=turned.at[row * COLS + col],
            dst_ref=back.at[my_slot],
            send_sem=send_sem.at[1],
            recv_sem=back_sem.at[pair],
            device_id=(row, col),
            device_id_type=MESH,
        ).start()
        return carry

    lax.fori_loop(1, DEVS, send_back, 0)

    def reduce_chunk(out, into, every, chunk, send, recv, recv_all):
        into[me] = out[chunk]
        wait_for(recv, into, DEVS - 1)

        def add(index, total):
            return total + jnp.sum(into[pl.ds(index * 16, 16)].astype(F32), axis=0)

        total = lax.fori_loop(0, DEVS // 16, add, jnp.zeros((16, CH), F32), unroll=True)
        every[chunk] = total.astype(BF)
        gather(every, chunk, send, recv_all)

    def grid_step(step, carry):
        tile = lax.rem(pair + TILES - step, TILES)
        wait_for(back_sem.at[tile], back, 16)
        slots = pl.ds(tile * 16, 16)
        mixed = from_slots(back[slots, 0:16, :].reshape(TILE, CH).astype(F32))
        d_mix = from_slots(back[slots, 16:32, :].reshape(TILE, CH).astype(F32))
        cot_bf = tile_of(cot, tile)
        n1 = n1_s[tile]
        outcome, d_branch = branch_post(
            mixed, d_mix, z_s[tile], n2_s[tile], r2_s[tile], gate_s[tile],
            slope2_s[tile, :, :CH], slope2_s[tile, :, CH:], mix_r_s[tile], mix_s[tile],
            d_gated_s[tile], up_s[tile], grid_in_ct, grid_out, a_grid_in, a_grid_out,
        )
        joined_s[tile, :, :CH] = outcome
        a_w_out[:CH, :] += dot_tn(outcome, cot_bf)
        d_first = (d_branch * slope1_s[tile]).astype(BF)
        a_w_in[:, :CH] += dot_tn(n1, d_first)
        d_first_s[tile, :, :CH] = d_first
        return carry

    def output_step(tile, carry):
        x_bf = tile_of(feat, tile)
        cot_bf = tile_of(cot, tile)
        n1 = n1_s[tile]
        at = pl.ds(pl.multiple_of(tile * 16, 16), 16)
        out = (x_bf.astype(F32) + dot(joined_s[tile], w_out[...])).astype(BF)
        result_v[:, at, :] = out.reshape(16, 16, CH)
        g = dot(d_first_s[tile], w_in_ct[...])
        unit = n1.astype(F32)
        grad = cot_bf.astype(F32) + r1_s[tile] * (g - unit * row_mean(g * unit))
        feature_grad_v[:, at, :] = grad.astype(BF).reshape(16, 16, CH)
        return carry

    def output_pair(index, carry):
        output_step(index * 2, 0)
        output_step(index * 2 + 1, 0)
        return carry

    def grid_pair(index, carry):
        grid_step(index * 2, 0)
        grid_step(index * 2 + 1, 0)
        return carry

    lax.fori_loop(0, TILES // 2, grid_pair, 0)
    at = pack(late_out, 0, a_grid_in[...])
    at = pack(late_out, at, a_grid_out[...])
    at = pack(late_out, at, a_w_out[:CH, :])
    pack(late_out, at, a_w_in[:, :CH])
    scatter(late_out, late_in, 0, LATE, send_sem.at[4], late_sem)

    lax.fori_loop(0, TILES // 2, output_pair, 0)
    result_out = pltpu.make_async_copy(result_v, result, io_sem.at[2])
    feature_grad_out = pltpu.make_async_copy(feature_grad_v, feature_grad, io_sem.at[3])
    result_out.start()
    feature_grad_out.start()

    @pl.when(mine < EARLY)
    def _():
        reduce_chunk(
            early_out, early_in, early_all, mine, send_sem.at[3], early_sem, early_all_sem
        )

    @pl.when(mine < LATE)
    def _():
        reduce_chunk(
            late_out, late_in, late_all, mine, send_sem.at[5], late_sem, late_all_sem
        )

    @pl.when(mine < EARLY)
    def _():
        wait_for(early_all_sem, early_all, EARLY - 1)
        wait_for(send_sem.at[2], early_out, EARLY - 1)

    @pl.when(mine >= EARLY)
    def _():
        wait_for(early_all_sem, early_all, EARLY)
        wait_for(send_sem.at[2], early_out, EARLY)

    early_copy = pltpu.make_async_copy(early_all, early_res, io_sem.at[0])
    early_copy.start()
    wait_for(send_sem.at[0], sent, DEVS - 1)
    wait_for(send_sem.at[1], turned, DEVS - 1)

    @pl.when(mine < EARLY)
    def _():
        wait_for(send_sem.at[3], early_in, DEVS - 1)

    @pl.when(mine >= LATE)
    def _():
        wait_for(late_all_sem, late_all, LATE)
        wait_for(send_sem.at[4], late_out, LATE)

    @pl.when(mine < LATE)
    def _():
        wait_for(late_all_sem, late_all, LATE - 1)
        wait_for(send_sem.at[4], late_out, LATE - 1)
        wait_for(send_sem.at[5], late_in, DEVS - 1)

    late_copy = pltpu.make_async_copy(late_all, late_res, io_sem.at[1])
    late_copy.start()
    early_copy.wait()
    late_copy.wait()
    result_out.wait()
    feature_grad_out.wait()


def unpack(src, at, shape):
    halves = []
    for _ in range(0, shape[1], CH):
        count = shape[0] // 16
        halves.append(src[at : at + count].reshape(shape[0], CH).astype(F32))
        at += count
    return jnp.concatenate(halves, axis=1) if len(halves) > 1 else halves[0]


def finish(
    result_in, feature_grad_in, early_in, late_in,
    result, feature_grad, o_w_in, o_grid_in, o_grid_mix, o_grid_out, o_block_in, o_block_mix,
    o_block_out, o_w_out, result_v, feature_grad_v, early_all, late_all, sem,
):
    arrivals = [
        pltpu.make_async_copy(result_in, result_v, sem.at[0]),
        pltpu.make_async_copy(feature_grad_in, feature_grad_v, sem.at[1]),
        pltpu.make_async_copy(early_in, early_all, sem.at[2]),
        pltpu.make_async_copy(late_in, late_all, sem.at[3]),
    ]
    copies = [
        pltpu.make_async_copy(result_v, result, sem.at[4]),
        pltpu.make_async_copy(feature_grad_v, feature_grad, sem.at[5]),
    ]
    for arrival in arrivals:
        arrival.start()
    for arrival, copy in zip(arrivals, copies):
        arrival.wait()
        copy.start()
    arrivals[2].wait()
    arrivals[3].wait()
    o_block_in[...] = unpack(early_all, 0, (128, 256))
    o_block_mix[...] = unpack(early_all, 16, (256, 256))
    o_block_out[...] = unpack(early_all, 48, (128, 128))
    o_w_out[CH:, :] = unpack(early_all, 56, (128, 128))
    o_w_in[:, CH:] = unpack(early_all, 64, (128, 128))
    o_grid_mix[...] = unpack(early_all, 72, (256, 256))
    o_grid_in[...] = unpack(late_all, 0, (128, 256))
    o_grid_out[...] = unpack(late_all, 16, (128, 128))
    o_w_out[:CH, :] = unpack(late_all, 24, (128, 128))
    o_w_in[:, :CH] = unpack(late_all, 32, (128, 128))
    for copy in copies:
        copy.wait()


def body(*args):
    def whole(dtype, *shape):
        return pltpu.VMEM(shape, dtype)

    pixels = (TILES, TILE, CH)
    both = (TILES, TILE, 2 * CH)
    scratch = [
        *[whole(BF, 16, 128, CH)] * 4,
        *[whole(BF, DEVS, 32, CH)] * 4,
        *[whole(BF, 256, 8 * CH)] * 4,
        whole(BF, *pixels),
        whole(F32, *pixels),
        whole(F32, *pixels),
        whole(BF, *pixels),
        whole(BF, *pixels),
        whole(F32, *pixels),
        whole(F32, *both),
        whole(F32, *pixels),
        whole(BF, *pixels),
        whole(F32, *pixels),
        whole(F32, *pixels),
        whole(BF, *pixels),
        whole(BF, *both),
        whole(BF, *both),
        *[whole(BF, TILE, TILE)] * 2,
        *[whole(BF, 2 * CH, CH)] * 3,
        *[whole(BF, 256, 256)] * 2,
        whole(BF, CH, 2 * CH),
        *[whole(BF, CH, CH)] * 2,
        whole(F32, CH, 2 * CH),
        whole(F32, CH, CH),
        whole(F32, CH, 2 * CH),
        whole(F32, 256, 256),
        whole(F32, CH, CH),
        whole(F32, CH, 2 * CH),
        whole(F32, 2 * CH, CH),
        whole(BF, EARLY, 16, CH),
        whole(BF, DEVS, 16, CH),
        whole(BF, EARLY, 16, CH),
        whole(BF, LATE, 16, CH),
        whole(BF, DEVS, 16, CH),
        whole(BF, LATE, 16, CH),
        pltpu.SemaphoreType.DMA((6,)),
        pltpu.SemaphoreType.DMA,
        pltpu.SemaphoreType.DMA((TILES,)),
        *[pltpu.SemaphoreType.DMA] * 4,
        pltpu.SemaphoreType.DMA((4,)),
    ]
    vmem = pl.BlockSpec(memory_space=pltpu.VMEM)
    shape = args[0].shape
    outs = [
        jax.ShapeDtypeStruct(shape, BF),
        jax.ShapeDtypeStruct(shape, BF),
        jax.ShapeDtypeStruct((128, 256), F32),
        jax.ShapeDtypeStruct((128, 256), F32),
        jax.ShapeDtypeStruct((256, 256), F32),
        jax.ShapeDtypeStruct((128, 128), F32),
        jax.ShapeDtypeStruct((128, 256), F32),
        jax.ShapeDtypeStruct((256, 256), F32),
        jax.ShapeDtypeStruct((128, 128), F32),
        jax.ShapeDtypeStruct((256, 128), F32),
    ]
    hbm = pl.BlockSpec(memory_space=pl.ANY)
    parts = pl.pallas_call(
        kernel,
        out_shape=[
            outs[0],
            outs[1],
            jax.ShapeDtypeStruct((EARLY, 16, CH), BF),
            jax.ShapeDtypeStruct((LATE, 16, CH), BF),
        ],
        in_specs=[hbm] * 2 + [vmem] * 8,
        out_specs=[hbm] * 4,
        scratch_shapes=scratch,
        compiler_params=pltpu.CompilerParams(
            collective_id=0, has_side_effects=True, vmem_limit_bytes=56 * 2**20
        ),
    )(*args)
    return tuple(
        pl.pallas_call(
            finish,
            out_shape=outs,
            in_specs=[hbm] * 4,
            out_specs=[hbm] * 2 + [vmem] * 8,
            scratch_shapes=[
                pltpu.VMEM(shape, BF),
                pltpu.VMEM(shape, BF),
                pltpu.VMEM(parts[2].shape, BF),
                pltpu.VMEM(parts[3].shape, BF),
                pltpu.SemaphoreType.DMA((6,)),
            ],
        )(*parts)
    )


def solution(mesh):
    split = P("row", "col", None)
    return jax.shard_map(
        body,
        mesh=mesh,
        in_specs=(split, split) + (P(),) * 8,
        out_specs=(split, split) + (P(),) * 8,
        check_vma=False,
    )
```
